32 devices in a mesh: seq: 2 (over x), span: 16 (over z, y, core).
Axes of the slice: x: 2, y: 2, z: 4, core: 2. Of those that a mesh axis runs over, the one named last changes fastest.
Arguments:
- tokens: bfloat16 [4, 1024, 2048], P('seq', 'span'), may hold values from -6 to 6
- doc_lengths: int32 [4, 4], P('seq'), may hold values from 0 to 1024, as said below
- ln1_gain: bfloat16 [2048], P(('seq', 'span')), may hold values from 0.5 to 1.5
- ln1_shift: bfloat16 [2048], P(('seq', 'span')), may hold values from -1.25 to 1.25
- q_weight: bfloat16 [2048, 2048], P(('seq', 'span')), may hold values from -0.125 to 0.125
- q_bias: bfloat16 [2048], P(('seq', 'span')), may hold values from -3 to 3
- kv_weight: bfloat16 [2048, 256], P(('seq', 'span')), may hold values from -0.125 to 0.125
- v_bias: bfloat16 [128], P(('seq', 'span')), may hold values from -0.3125 to 0.3125
- o_weight: bfloat16 [2048, 2048], P(('seq', 'span')), may hold values from -2 to 2
- o_bias: bfloat16 [2048], P(('seq', 'span')), may hold values from -3 to 3
- ln2_gain: bfloat16 [2048], P(('seq', 'span')), may hold values from 0.5 to 1.5
- ln2_shift: bfloat16 [2048], P(('seq', 'span')), may hold values from -1.25 to 1.25
- fc_weight: bfloat16 [2048, 8192], P(('seq', 'span')), may hold values from -0.125 to 0.125
- fc_bias: bfloat16 [8192], P(('seq', 'span')), may hold values from -3 to 3
- proj_weight: bfloat16 [8192, 2048], P(('seq', 'span')), may hold values from -0.0625 to 0.0625
- proj_bias: bfloat16 [2048], P(('seq', 'span')), may hold values from -3 to 3
- cotangent: bfloat16 [4, 1024, 2048], P('seq', 'span'), may hold values from -6 to 6
Outputs:
- output: bfloat16 [4, 1024, 2048], P('seq', 'span')
- input_grad: float32 [4, 1024, 2048], P('seq', 'span')
- ln1_gain_grad: float32 [2048], P(('seq', 'span'))
- ln1_shift_grad: float32 [2048], P(('seq', 'span'))
- q_weight_grad: float32 [2048, 2048], P(('seq', 'span'))
- q_bias_grad: float32 [2048], P(('seq', 'span'))
- kv_weight_grad: float32 [2048, 256], P(('seq', 'span'))
- v_bias_grad: float32 [128], P(('seq', 'span'))
- o_weight_grad: float32 [2048, 2048], P(('seq', 'span'))
- o_bias_grad: float32 [2048], P(('seq', 'span'))
- ln2_gain_grad: float32 [2048], P(('seq', 'span'))
- ln2_shift_grad: float32 [2048], P(('seq', 'span'))
- fc_weight_grad: float32 [2048, 8192], P(('seq', 'span'))
- fc_bias_grad: float32 [8192], P(('seq', 'span'))
- proj_weight_grad: float32 [8192, 2048], P(('seq', 'span'))
- proj_bias_grad: float32 [2048], P(('seq', 'span'))
The draws below stay inside these ranges and needn't reach their ends.
Inputs may be any that keep to these rules, and one draw needn't show every extreme that they name: `doc_lengths`: each row sums to 1024. In each group of 2 consecutive rows one row, drawn from the seed, is a single document: 1024 followed by zeros. Other rows may hold empty documents.
All inputs are finite; a program needn't handle non-finite values.
Results may differ from the reference program's by a relative error of at most 0.013.
Values may be sent and summed in bfloat16 or wider, within the bound.
No kernel may reach another device: no remote copies, remote signals or barrier semaphores. Data moves between devices by JAX's collectives and lax.ppermute only.
A program may use at most 448 MiB of HBM per device.

```python
import jax
import jax.numpy as jnp
from jax import lax

HEADS = 16
HD = 128
D = 2048
FF = 8192
SEQS = 2
DOCS = 4
SEQ_LEN = 1024
SEQUENCES = 4


def draw_doc_lengths(key, part):
    whole_key, cut_key = jax.random.split(jax.random.fold_in(key, 11))
    groups = SEQUENCES // SEQS
    chosen = jax.random.randint(whole_key, (groups, 1), 0, SEQS)
    cuts = jnp.sort(jax.random.randint(cut_key, (SEQUENCES, DOCS - 1), 0, SEQ_LEN + 1), axis=1)
    edges = jnp.concatenate([jnp.zeros((SEQUENCES, 1), jnp.int32), cuts, jnp.full((SEQUENCES, 1), SEQ_LEN, jnp.int32)], axis=1)
    ragged = edges[:, 1:] - edges[:, :-1]
    single = jnp.concatenate([jnp.full((SEQUENCES, 1), SEQ_LEN, jnp.int32), jnp.zeros((SEQUENCES, DOCS - 1), jnp.int32)], axis=1)
    picked = jnp.arange(SEQUENCES, dtype=jnp.int32).reshape(groups, SEQS) == chosen
    return jnp.where(picked.reshape(SEQUENCES, 1), single, ragged).astype(jnp.int32)


def strengthened(entries, rng, source, target, blocks, factor):
    owner, partner = [(jnp.arange(entries.shape[position]) // (entries.shape[position] // blocks)).reshape([-1 if axis == position else 1 for axis in range(entries.ndim)]) for position in (source, target)]
    chosen = jax.random.permutation(rng, blocks)[partner]
    strong = (owner == chosen) | (owner == (partner + blocks // 2) % blocks)
    return jnp.where(strong, factor * entries, entries)


def levels(key, shape, shards, smallest, high):
    loudness = 1.0
    for dim, blocks in shards:
        heights = jax.random.uniform(jax.random.fold_in(jax.random.fold_in(key, 6), dim), (blocks,), jnp.float32, smallest / len(shards), high / len(shards))
        loudness = loudness * jnp.repeat(jnp.exp(heights), shape[dim] // blocks).reshape((-1,) + (1,) * (len(shape) - 1 - dim))
    return loudness


def bell_draw(key, shape, scale, reach, cuts=(), kind=jnp.bfloat16):
    drawn = jax.random.normal(key, shape, jnp.float32) * scale
    if len(cuts) > 0:
        drawn = levels(key, shape, cuts, -0.22, 0.18) * drawn
    return jnp.clip(drawn, min=-reach, max=reach).astype(kind)


def heavy_noise(stream_key, dims, width, bound, shards, heavy, kind=jnp.bfloat16):
    values = width * jax.random.normal(stream_key, dims, jnp.float32)
    if shards:
        values = values * levels(stream_key, dims, shards, -0.22, 0.18)
    return jnp.clip(strengthened(values, jax.random.fold_in(stream_key, 3), *heavy), -bound, bound).astype(kind)


def setup_inputs(seed: int = 0) -> dict:
    arg_keys = jax.random.split(jax.random.key(seed), 18)
    return {
        "tokens": heavy_noise(arg_keys[0], (SEQUENCES, SEQ_LEN, D), 1.0, 6.0, ((0, 2), (1, 16)), (1, 2, 16, 2.0)),
        "doc_lengths": draw_doc_lengths(jax.random.fold_in(arg_keys[17], 71), 0),
        "ln1_gain": jnp.clip(1.0 + 0.1 * jax.random.normal(arg_keys[2], (D,), jnp.float32), 0.5, 1.5).astype(jnp.bfloat16),
        "ln1_shift": bell_draw(arg_keys[3], (D,), 0.2, 1.25, ((0, 32),)),
        "q_weight": bell_draw(arg_keys[4], (D, D), D ** -0.5, 0.125, ((0, 32),)),
        "q_bias": bell_draw(arg_keys[5], (D,), 0.5, 3.0, ((0, 32),)),
        "kv_weight": bell_draw(arg_keys[6], (D, 2 * HD), D ** -0.5, 0.125, ((0, 32),)),
        "v_bias": bell_draw(arg_keys[7], (HD,), 0.05, 0.3125, ((0, 32),)),
        "o_weight": bell_draw(arg_keys[8], (D, D), (max(D // 256, 2)) ** -0.5, 2.0, ((0, 32),)),
        "o_bias": bell_draw(arg_keys[9], (D,), 0.5, 3.0, ((0, 32),)),
        "ln2_gain": jnp.clip(1.0 + 0.1 * jax.random.normal(arg_keys[10], (D,), jnp.float32), 0.5, 1.5).astype(jnp.bfloat16),
        "ln2_shift": bell_draw(arg_keys[11], (D,), 0.2, 1.25, ((0, 32),)),
        "fc_weight": bell_draw(arg_keys[12], (D, FF), D ** -0.5, 0.125, ((0, 32),)),
        "fc_bias": bell_draw(arg_keys[13], (FF,), 0.5, 3.0, ((0, 32),)),
        "proj_weight": bell_draw(arg_keys[14], (FF, D), FF ** -0.5, 0.0625, ((0, 32),)),
        "proj_bias": bell_draw(arg_keys[15], (D,), 0.5, 3.0, ((0, 32),)),
        "cotangent": heavy_noise(arg_keys[16], (SEQUENCES, SEQ_LEN, D), 1.0, 6.0, ((0, 2), (1, 16)), (1, 2, 16, 2.0)),
    }


EPS = 1e-05
GELU_C = 0.7978845608028654
MASKED = -1e+30
HIGH = lax.Precision.HIGHEST

@jax.custom_vjp
def low(v):
    return lax.optimization_barrier(v.astype(jnp.bfloat16)).astype(jnp.float32)

@jax.custom_vjp
def low_back(v):
    return v

def low_keep(v):
    return (low(v), None)

def low_pass(kept, grad):
    return (grad,)

def back_keep(v):
    return (v, None)

def back_low(kept, grad):
    return (low(grad),)
low.defvjp(low_keep, low_pass)
low_back.defvjp(back_keep, back_low)

def layer_norm(values, gain, shift):
    center = values - lax.optimization_barrier(jnp.mean(values, axis=-1, keepdims=True))
    spread = lax.optimization_barrier(jnp.mean(center * center, axis=-1, keepdims=True))
    return center * lax.rsqrt(spread + EPS) * gain + shift

def gelu_tanh(values):
    return 0.5 * values * (1.0 + jnp.tanh(GELU_C * (values + 0.044715 * values * values * values)))

def attention(queries, key_rows, value_rows, doc_sizes):
    length = key_rows.shape[0]
    q_block = min(length, 512)
    doc_ends = jnp.cumsum(doc_sizes).astype(jnp.int32)
    positions = jnp.arange(length, dtype=jnp.int32)
    key_docs = lax.optimization_barrier(jnp.sum((positions[:, None] >= doc_ends[None, :]).astype(jnp.int32), axis=1))

    def one_block(block_item):
        block_start, block_rows = block_item
        scores = jnp.einsum('bhe,ke->bhk', block_rows, key_rows, precision=HIGH) * HD ** (-0.5)
        scores = low_back(scores)
        query_pos = block_start + jnp.arange(q_block, dtype=jnp.int32)
        query_docs = lax.optimization_barrier(jnp.sum((query_pos[:, None] >= doc_ends[None, :]).astype(jnp.int32), axis=1))
        visible = (positions[None, :] <= query_pos[:, None]) & (key_docs[None, :] == query_docs[:, None])
        scores = jnp.where(visible[:, None, :], scores, MASKED)
        row_max = lax.optimization_barrier(jnp.max(scores, axis=-1, keepdims=True))
        exponent = jnp.exp(scores - row_max)
        probs = low(exponent / lax.optimization_barrier(jnp.sum(exponent, axis=-1, keepdims=True)))
        return jnp.einsum('bhk,ke->bhe', probs, value_rows, precision=HIGH)
    block_starts = jnp.arange(length // q_block, dtype=jnp.int32) * q_block
    blocks = queries.reshape(length // q_block, q_block, HEADS, HD)
    mixed = lax.map(jax.checkpoint(one_block), (block_starts, blocks))
    return mixed.reshape(length, HEADS * HD)

def sequence_forward(seq_rows, doc_sizes, ln1_gain, ln1_shift, q_weight, q_bias, kv_weight, v_bias, o_weight, o_bias, ln2_gain, ln2_shift, fc_weight, fc_bias, proj_weight, proj_bias):
    normed_one = low(layer_norm(seq_rows, ln1_gain, ln1_shift))
    queries = low(low_back(jnp.dot(normed_one, q_weight, precision=HIGH) + q_bias))
    pair_shift = jnp.concatenate([jnp.zeros_like(v_bias), v_bias])
    pairs = low(low_back(jnp.dot(normed_one, kv_weight, precision=HIGH) + pair_shift))
    key_rows = pairs[:, :HD]
    value_rows = pairs[:, HD:]
    mixed = low(low_back(attention(queries.reshape(-1, HEADS, HD), key_rows, value_rows, doc_sizes)))
    resid = seq_rows + low_back(jnp.dot(mixed, o_weight, precision=HIGH) + o_bias)
    normed_two = low(layer_norm(resid, ln2_gain, ln2_shift))
    pre_act = low_back(jnp.dot(normed_two, fc_weight, precision=HIGH) + fc_bias)
    activation = low(gelu_tanh(pre_act))
    return resid + jnp.dot(activation, proj_weight, precision=HIGH) + proj_bias

def reference(tokens, doc_lengths, ln1_gain, ln1_shift, q_weight, q_bias, kv_weight, v_bias, o_weight, o_bias, ln2_gain, ln2_shift, fc_weight, fc_bias, proj_weight, proj_bias, cotangent):
    params = tuple((param.astype(jnp.float32) for param in (ln1_gain, ln1_shift, q_weight, q_bias, kv_weight, v_bias, o_weight, o_bias, ln2_gain, ln2_shift, fc_weight, fc_bias, proj_weight, proj_bias)))

    def accumulate(totals, sequence):
        seq_rows, doc_sizes, seq_cot = sequence

        def forward_fn(rows_in, *weights):
            return sequence_forward(rows_in, doc_sizes, *weights)
        result, pullback = jax.vjp(forward_fn, seq_rows.astype(jnp.float32), *params)
        gradients = pullback(seq_cot.astype(jnp.float32))
        new_totals = tuple((total + grad for total, grad in zip(totals, gradients[1:])))
        return (new_totals, (result.astype(jnp.bfloat16), gradients[0]))
    zeros = tuple((jnp.zeros_like(param) for param in params))
    totals, (output, input_grad) = lax.scan(accumulate, zeros, (tokens, doc_lengths, cotangent))
    return (output, input_grad, totals[0], totals[1], totals[2], totals[3], totals[4], totals[5], totals[6], totals[7], totals[8], totals[9], totals[10], totals[11], totals[12], totals[13])
```

```python
import math

import jax
import jax.numpy as jnp
from jax import lax
from jax.sharding import Mesh
from jax.sharding import PartitionSpec as P

HEADS = 16
HD = 128

EPS = 1e-05
GELU_C = 0.7978845608028654
MASKED = -1e30
FLOOR_MAX = -1e29
LOW = jnp.bfloat16
F32 = jnp.float32
SWAP = [(0, 1), (1, 0)]


def layer_norm(values, gain, shift):
    center = values - jnp.mean(values, axis=-1, keepdims=True)
    spread = jnp.mean(center * center, axis=-1, keepdims=True)
    return center * lax.rsqrt(spread + EPS) * gain + shift


def gelu_tanh(values):
    return 0.5 * values * (1.0 + jnp.tanh(GELU_C * (values + 0.044715 * values * values * values)))


def doc_number(doc_ends, positions):
    return jnp.sum((positions[None, :, None] >= doc_ends[:, None, :]).astype(jnp.int32), axis=-1)


def dot(left, right, dims=((1,), (0,))):
    return lax.dot_general(left, right, (dims, ((), ())), preferred_element_type=F32)


def swap(value, axis):
    return lax.ppermute(value, axis, SWAP)


def add_low(own, got):
    return (own.astype(F32) + got.astype(F32)).astype(LOW)


def in_order(own, got, axis, at=0):
    first = lax.axis_index(axis) == 0
    return jnp.stack([jnp.where(first, own, got), jnp.where(first, got, own)], axis=at)


def own_other(value, axis, at):
    index = lax.axis_index(axis)
    own = lax.dynamic_index_in_dim(value, index, at, keepdims=False)
    other = lax.dynamic_index_in_dim(value, 1 - index, at, keepdims=False)
    return own, other


def gather_two(value, axis, at=0):
    return in_order(value, swap(value, axis), axis, at)


def shift_z(value, by):
    count = lax.axis_size("z")
    return lax.ppermute(value, "z", [(i, (i + by) % count) for i in range(count)])


def gather_z(value, direct):
    count = lax.axis_size("z")
    me = lax.axis_index("z")
    held = [value]
    for step in range(1, count):
        held.append(shift_z(value, step) if direct else shift_z(held[-1], 1))
    held = jnp.stack(held)
    return jnp.stack(
        [lax.dynamic_index_in_dim(held, (me - a) % count, 0, keepdims=False) for a in range(count)]
    )


def scatter_z(value, low=True):
    count = lax.axis_size("z")
    me = lax.axis_index("z")

    def mine(step):
        return lax.dynamic_index_in_dim(value, (me - step) % count, 0, keepdims=False)

    running = mine(1)
    for step in range(2, count + 1):
        got = shift_z(running, 1)
        running = mine(step).astype(F32) + got.astype(F32)
        if step < count and low:
            running = running.astype(LOW)
    return running


def gather_chips(value):
    half = value.shape[1] // 2
    left = gather_z(value[:, :half], False)
    right = gather_z(value[:, half:], False)
    left = gather_two(gather_two(left, "x", 0), "y", 2)
    right = gather_two(gather_two(right, "y", 1), "x", 0)
    return jnp.concatenate([left, right], axis=-1)


def gather_rows(value):
    chips = gather_chips(value)
    whole = gather_two(chips, "c", 3)
    return whole.reshape(-1, value.shape[1])


def gather_rows_small(value):
    whole = gather_z(value, True)
    whole = gather_two(whole, "y", 1)
    whole = gather_two(whole, "x", 0)
    whole = gather_two(whole, "c", 3)
    return whole


def scatter_rows(value):
    count = lax.axis_size("z")
    width = value.shape[1]
    value = value.reshape(2, count, 2, 2, -1, width)
    own, other = own_other(value, "c", 3)
    value = add_low(own, swap(other, "c"))
    left, right = value[..., : width // 2], value[..., width // 2 :]
    own, other = own_other(left, "x", 0)
    left = add_low(own, swap(other, "x"))
    own, other = own_other(right, "y", 2)
    right = add_low(own, swap(other, "y"))
    own, other = own_other(left, "y", 1)
    left = add_low(own, swap(other, "y"))
    own, other = own_other(right, "x", 0)
    right = add_low(own, swap(other, "x"))
    return jnp.concatenate([scatter_z(left), scatter_z(right)], axis=-1)


def scatter_small(value):
    count = lax.axis_size("z")
    value = value.reshape(2, count, 2, 2, -1)
    for axis, at in (("c", 3), ("y", 2), ("x", 0)):
        own, other = own_other(value, axis, at)
        value = own + swap(other, axis)
    return scatter_z(value, False)


def spread_columns(value):
    own, other = own_other(value, "c", 3)
    value = gather_in(own, other, "c")
    own, other = own_other(value, "y", 3)
    value = gather_in(own, other, "y")
    own, other = own_other(value, "x", 3)
    return gather_in(own, other, "x")


def gather_in(own, other, axis):
    return in_order(own, swap(other, axis), axis)


def collect_columns(value):
    own, other = own_other(value, "x", 0)
    value = in_order(own, swap(other, "x"), "x", 3)
    own, other = own_other(value, "y", 0)
    value = in_order(own, swap(other, "y"), "y", 3)
    own, other = own_other(value, "c", 0)
    return in_order(own, swap(other, "c"), "c", 3)


def gather_plane(value):
    half = value.shape[0] // 2
    left, right = value[:half], value[half:]
    left_x, right_y = swap(left, "x"), swap(right, "y")
    left_two = jnp.concatenate([left, left_x])
    right_two = jnp.concatenate([right, right_y])
    four = jnp.concatenate([left_two, swap(left_two, "y"), right_two, swap(right_two, "x")])
    return jnp.concatenate([four, swap(four, "c")])


def scatter_plane(value):
    rows = value.shape[0] // 2
    four = add_low(value[:rows], swap(value[rows:], "c"))
    part = rows // 4
    left_own, left_far = four[:part], four[part : 2 * part]
    right_own, right_far = four[2 * part : 3 * part], four[3 * part :]
    left = add_low(left_own, swap(left_far, "y"))
    right = add_low(right_own, swap(right_far, "x"))
    half = part // 2
    left = left[:half].astype(F32) + swap(left[half:], "x").astype(F32)
    right = right[:half].astype(F32) + swap(right[half:], "y").astype(F32)
    return jnp.concatenate([left, right])


def masked_scores(queries, key_rows, query_pos, query_doc, doc_ends, key_start):
    count = key_rows.shape[1]
    scores = jnp.einsum(
        "sche,sre->schr", queries, key_rows, preferred_element_type=F32
    ) * HD ** (-0.5)
    key_pos = key_start + jnp.arange(count, dtype=jnp.int32)
    key_doc = doc_number(doc_ends, key_pos)
    visible = (key_pos[None, None, :] <= query_pos[None, :, None]) & (
        key_doc[:, None, :] == query_doc[:, :, None]
    )
    return jnp.where(visible[:, :, None, :], scores, MASKED)


def local_fold(step, initial, buffer):
    length = buffer.shape[1]
    block_rows = math.gcd(length, 512)

    def turn(index, carried):
        block_start = index * block_rows
        piece = lax.dynamic_slice_in_dim(buffer, block_start, block_rows, 1)
        return step(carried, piece, block_start)

    return lax.fori_loop(0, length // block_rows, turn, initial)


def local(
    tokens,
    doc_lengths,
    ln1_gain,
    ln1_shift,
    q_weight,
    q_bias,
    kv_weight,
    v_bias,
    o_weight,
    o_bias,
    ln2_gain,
    ln2_shift,
    fc_weight,
    fc_bias,
    proj_weight,
    proj_bias,
    cotangent,
):
    seqs_here, span_rows, width = tokens.shape
    row_count = seqs_here * span_rows
    planes = lax.axis_size("z")
    devices = 8 * planes
    rows = q_weight.shape[0]
    hidden = proj_weight.shape[0]
    span_size = 4 * planes
    at_x, at_z, at_y, at_c = (lax.axis_index(name) for name in ("x", "z", "y", "c"))
    span_index = at_z * 4 + at_y * 2 + at_c

    small = (ln1_gain, ln1_shift, q_bias, o_bias, ln2_gain, ln2_shift, proj_bias, fc_bias, v_bias)
    flat = jnp.concatenate(small)
    lanes = kv_weight.shape[1]
    flat = jnp.pad(flat, (0, -flat.shape[0] % (16 * lanes))).reshape(-1, lanes)
    packed = gather_rows_small(jnp.concatenate([kv_weight, flat]))
    pair_w = packed[..., :rows, :].reshape(width, lanes)
    flat = packed[..., rows:, :].reshape(devices, -1)
    parts, start = [], 0
    for piece in small:
        parts.append(flat[:, start : start + piece.shape[0]].reshape(-1).astype(F32))
        start += piece.shape[0]
    gain_one, shift_one, query_b, out_b, gain_two, shift_two, down_b, up_b, value_b = parts
    up_b = up_b.reshape(2, planes, 2, 2, hidden)
    up_b = lax.dynamic_slice(
        up_b, (at_x, 0, at_y, at_c, 0), (1, planes, 1, 1, hidden)
    ).reshape(-1)

    query_w = gather_rows(q_weight)
    out_w = gather_rows(o_weight)

    up_own = fc_weight.reshape(rows, 2, planes, 2, 2, hidden).transpose(0, 1, 3, 4, 2, 5)
    up_own = spread_columns(up_own.reshape(rows, 2, 2, 2, planes * hidden))
    up_own = up_own.reshape(2, 4 * rows, planes * hidden)
    up_w = lax.all_gather(up_own, "z", axis=1, tiled=True).reshape(width, planes * hidden)
    down_w = lax.all_gather(proj_weight, "z", axis=0, tiled=True)

    grad_out = cotangent.reshape(row_count, width)
    grad_out_plane = gather_plane(grad_out)

    query_pos = span_index * span_rows + jnp.arange(span_rows, dtype=jnp.int32)
    last_query = span_index * span_rows + span_rows - 1
    doc_ends = jnp.stack(
        [jnp.sum(doc_lengths[:, : j + 1], axis=1) for j in range(doc_lengths.shape[1])], axis=1
    )
    query_doc = doc_number(doc_ends, query_pos)
    inputs_float = tokens.reshape(row_count, width).astype(F32)
    normed_one_f, norm_pull_one = jax.vjp(layer_norm, inputs_float, gain_one, shift_one)
    normed_one = normed_one_f.astype(LOW)
    pair_shift = jnp.concatenate([jnp.zeros((HD,), F32), value_b])
    pairs = (dot(normed_one, pair_w) + pair_shift).astype(LOW)
    kv_whole = gather_z(pairs.reshape(seqs_here, span_rows, 2 * HD), True)
    kv_whole = gather_two(gather_two(kv_whole, "y", 1), "c", 2)
    kv_whole = jnp.moveaxis(kv_whole, 3, 0).reshape(seqs_here, span_size * span_rows, 2 * HD)
    queries = (dot(normed_one, query_w) + query_b).astype(LOW)
    queries = queries.reshape(seqs_here, span_rows, HEADS, HD)

    def lse_step(carried, piece, piece_start):

        def lse_compute(state_in):
            running, total = state_in
            scores = masked_scores(
                queries, piece[:, :, :HD], query_pos, query_doc, doc_ends, piece_start
            )
            fresh = jnp.maximum(running, jnp.max(scores, axis=-1))
            total = total * jnp.exp(running - fresh) + jnp.sum(
                jnp.exp(scores - fresh[..., None]), axis=-1
            )
            return (fresh, total)

        return lax.cond(piece_start <= last_query, lse_compute, lambda state_in: state_in, carried)

    def out_step(carried, piece, piece_start):

        def out_compute(summed):
            scores = masked_scores(
                queries, piece[:, :, :HD], query_pos, query_doc, doc_ends, piece_start
            )
            probs = jnp.exp(scores - log_total[..., None]).astype(LOW)
            return summed + jnp.einsum(
                "schr,sre->sche", probs, piece[:, :, HD:], preferred_element_type=F32
            )

        return lax.cond(piece_start <= last_query, out_compute, lambda summed: summed, carried)

    stat_shape = (seqs_here, span_rows, HEADS)
    lse_init = (jnp.full(stat_shape, FLOOR_MAX, F32), jnp.zeros(stat_shape, F32))
    out_init = jnp.zeros((seqs_here, span_rows, HEADS, HD), F32)
    running, total = local_fold(lse_step, lse_init, kv_whole)
    log_total = running + jnp.log(total)
    attn_float = local_fold(out_step, out_init, kv_whole)
    attn_low = attn_float.reshape(row_count, width).astype(LOW)
    resid = inputs_float + dot(attn_low, out_w) + out_b

    normed_two_f, norm_pull_two = jax.vjp(layer_norm, resid, gain_two, shift_two)
    normed_plane = gather_plane(normed_two_f.astype(LOW))
    pre_act = dot(normed_plane, up_w) + up_b
    active_f, gelu_pull = jax.vjp(gelu_tanh, pre_act)
    activation = active_f.astype(LOW)
    grad_down_w = dot(activation, grad_out_plane, ((0,), (0,))).astype(LOW)
    grad_down_w = lax.psum_scatter(grad_down_w, "z", scatter_dimension=0, tiled=True).astype(F32)
    grad_active = dot(grad_out_plane, down_w, ((1,), (1,)))
    grad_pre = gelu_pull(grad_active)[0].astype(LOW)
    grad_normed_two = scatter_plane(dot(grad_pre, up_w, ((1,), (1,))).astype(LOW))
    grad_up_w = dot(normed_plane, grad_pre, ((0,), (0,))).astype(LOW)
    grad_up_w = lax.psum_scatter(
        grad_up_w.reshape(2, planes * 4 * rows, planes * hidden),
        "z",
        scatter_dimension=1,
        tiled=True,
    )
    grad_up_w = collect_columns(grad_up_w.reshape(2, 2, 2, rows, planes * hidden))
    grad_up_w = (
        grad_up_w.reshape(rows, 2, 2, 2, planes, hidden)
        .transpose(0, 1, 4, 2, 3, 5)
        .reshape(rows, -1)
        .astype(F32)
    )
    grad_up_b = jnp.sum(grad_pre.astype(F32), axis=0)
    output = (resid + scatter_plane(dot(activation, down_w).astype(LOW)) + down_b).astype(LOW)
    grad_down_b = jnp.sum(grad_out.astype(F32), axis=0)

    grad_resid_part, grad_gain_two, grad_shift_two = norm_pull_two(grad_normed_two)
    grad_resid = grad_out.astype(F32) + grad_resid_part
    grad_proj = grad_resid.astype(LOW)

    grad_out_w = scatter_rows(dot(attn_low, grad_proj, ((0,), (0,))).astype(LOW))
    grad_out_b = jnp.sum(grad_proj.astype(F32), axis=0)
    grad_heads = dot(grad_proj, out_w, ((1,), (1,))).astype(LOW)
    grad_heads = grad_heads.reshape(seqs_here, span_rows, HEADS, HD)
    delta = jnp.sum(grad_heads.astype(F32) * attn_float, axis=-1)

    def back_step(carried, piece, piece_start):

        def back_compute(state_in):
            grad_query, grad_pairs = state_in
            key_rows = piece[:, :, :HD]
            value_rows = piece[:, :, HD:]
            scores = masked_scores(queries, key_rows, query_pos, query_doc, doc_ends, piece_start)
            probs = jnp.exp(scores - log_total[..., None])
            grad_values = jnp.einsum(
                "schr,sche->sre", probs.astype(LOW), grad_heads, preferred_element_type=F32
            )
            grad_probs = jnp.einsum(
                "sche,sre->schr", grad_heads, value_rows, preferred_element_type=F32
            )
            grad_scores = (probs * (grad_probs - delta[..., None])).astype(LOW)
            grad_query = grad_query + jnp.einsum(
                "schr,sre->sche", grad_scores, key_rows, preferred_element_type=F32
            ) * HD ** (-0.5)
            grad_keys = jnp.einsum(
                "schr,sche->sre", grad_scores, queries, preferred_element_type=F32
            ) * HD ** (-0.5)
            update = jnp.concatenate([grad_keys, grad_values], axis=-1)
            current = lax.dynamic_slice_in_dim(grad_pairs, piece_start, piece.shape[1], 1)
            grad_pairs = lax.dynamic_update_slice_in_dim(
                grad_pairs, current + update, piece_start, 1
            )
            return (grad_query, grad_pairs)

        return lax.cond(piece_start <= last_query, back_compute, lambda state_in: state_in, carried)

    back_init = (
        jnp.zeros((seqs_here, span_rows, HEADS, HD), F32),
        jnp.zeros((seqs_here, span_size * span_rows, 2 * HD), F32),
    )
    grad_query, grad_pairs = local_fold(back_step, back_init, kv_whole)
    grad_pairs = grad_pairs.reshape(seqs_here, planes, 2, 2, span_rows, 2 * HD)
    own, other = own_other(grad_pairs, "c", 3)
    grad_pairs = own + swap(other.astype(LOW), "c").astype(F32)
    own, other = own_other(grad_pairs, "y", 2)
    grad_pairs = own + swap(other.astype(LOW), "y").astype(F32)
    own_pairs = scatter_z(jnp.moveaxis(grad_pairs, 1, 0).astype(LOW))
    own_pairs = own_pairs.astype(LOW).reshape(row_count, 2 * HD)
    query_grad_low = grad_query.reshape(row_count, width).astype(LOW)
    grad_query_w = scatter_rows(dot(normed_one, query_grad_low, ((0,), (0,))).astype(LOW))
    grad_query_b = jnp.sum(query_grad_low.astype(F32), axis=0)
    grad_pair_w = scatter_rows(dot(normed_one, own_pairs, ((0,), (0,))).astype(LOW))
    grad_value_b = jnp.sum(own_pairs[:, HD:].astype(F32), axis=0)
    grad_normed_one = dot(query_grad_low, query_w, ((1,), (1,))) + dot(
        own_pairs, pair_w, ((1,), (1,))
    )
    grad_input_part, grad_gain_one, grad_shift_one = norm_pull_one(grad_normed_one)
    input_grad = grad_resid + grad_input_part

    grad_up_whole = lax.dynamic_update_slice(
        jnp.zeros((2, planes, 2, 2, hidden), F32),
        grad_up_b.reshape(1, planes, 1, 1, hidden),
        (at_x, 0, at_y, at_c, 0),
    ).reshape(-1)
    vectors = (
        grad_gain_one,
        grad_shift_one,
        grad_query_b,
        grad_out_b,
        grad_gain_two,
        grad_shift_two,
        grad_down_b,
        grad_up_whole,
        grad_value_b,
    )
    flat = jnp.concatenate([vector.reshape(devices, -1) for vector in vectors], axis=1)
    size = flat.shape[1]
    flat = scatter_small(jnp.pad(flat, ((0, 0), (0, -size % 128))))
    sums, start = [], 0
    for piece in small:
        sums.append(flat[start : start + piece.shape[0]])
        start += piece.shape[0]
    return (
        output.reshape(seqs_here, span_rows, width),
        input_grad.reshape(seqs_here, span_rows, width),
        sums[0],
        sums[1],
        grad_query_w,
        sums[2],
        grad_pair_w,
        sums[8],
        grad_out_w,
        sums[3],
        sums[4],
        sums[5],
        grad_up_w,
        sums[7],
        grad_down_w,
        sums[6],
    )


def solution(mesh):
    span = mesh.shape["span"]
    fine = Mesh(mesh.devices.reshape(2, span // 4, 2, 2), ("x", "z", "y", "c"))
    every = ("x", "z", "y", "c")
    acts = P("x", ("z", "y", "c"), None)
    vector = P(every)
    matrix = P(every, None)
    return jax.shard_map(
        local,
        mesh=fine,
        in_specs=(
            acts,
            P("x", None),
            vector,
            vector,
            matrix,
            vector,
            matrix,
            vector,
            matrix,
            vector,
            vector,
            vector,
            matrix,
            vector,
            matrix,
            vector,
            acts,
        ),
        out_specs=(
            acts,
            acts,
            vector,
            vector,
            matrix,
            vector,
            matrix,
            vector,
            matrix,
            vector,
            vector,
            vector,
            matrix,
            vector,
            matrix,
            vector,
        ),
        check_vma=False,
    )
```

```python
import itertools

import jax
import jax.numpy as jnp
from jax import lax
from jax.experimental import pallas as pl
from jax.experimental.pallas import tpu as pltpu
from jax.sharding import Mesh
from jax.sharding import PartitionSpec as P

HEADS = 16
HD = 128

EPS = 1e-05
GELU_C = 0.7978845608028654
MASKED = -1e30
LOG2E = 1.4426950408889634
LOW = jnp.bfloat16
F32 = jnp.float32
SWAP = [(0, 1), (1, 0)]


def layer_norm(values, gain, shift):
    center = values - jnp.mean(values, axis=-1, keepdims=True)
    spread = jnp.mean(center * center, axis=-1, keepdims=True)
    return center * lax.rsqrt(spread + EPS) * gain + shift


def gelu_tanh(values):
    return 0.5 * values * (1.0 + jnp.tanh(GELU_C * (values + 0.044715 * values * values * values)))


def dot(left, right, dims=((1,), (0,))):
    return lax.dot_general(left, right, (dims, ((), ())), preferred_element_type=F32)


def swap(value, axis):
    return lax.ppermute(value, axis, SWAP)


def add_low(own, got):
    return (own.astype(F32) + got.astype(F32)).astype(LOW)


CHIPS = ("x", "y")
LINE = ("z", "c")
PLANE = ("x", "y", "c")
EVERY = ("x", "z", "y", "c")


def exchange(value, axes):
    return lax.all_to_all(value, axes, 0, 0, tiled=True)


def spread(value, axes):
    return exchange(jnp.broadcast_to(value, (lax.axis_size(axes), *value.shape)), axes)


def after(value, *events):
    return lax.optimization_barrier((value, *events))[0]


def hop(value, mask):
    return lax.ppermute(value, CHIPS, [(i, i ^ mask) for i in range(4)])


def pick_blocks(value, order):
    size = value.shape[1] // len(order)
    if size % HD:
        return jnp.concatenate([value[:, i * size : (i + 1) * size] for i in order], axis=1)

    def kernel(in_ref, out_ref):
        for to, i in enumerate(order):
            out_ref[:, to * size : (to + 1) * size] = in_ref[:, i * size : (i + 1) * size]

    shape = jax.ShapeDtypeStruct(value.shape, value.dtype)
    return pl.pallas_call(kernel, out_shape=shape, name="pick_blocks")(value)


def spread_heads(value, planes):
    rows = value.shape[0]

    def kernel(in_ref, out_ref):
        for x, y, c, two in itertools.product((0, 1), repeat=4):
            start = (((x * 2 + c) * 2 + two) * 2 + y) * HD
            piece = in_ref[:, start : start + HD]
            for z in range(planes):
                target = ((x * planes + z) * 2 + y) * 2 + c
                out_ref[target, :, two * HD : (two + 1) * HD] = piece

    shape = jax.ShapeDtypeStruct((8 * planes, rows, 2 * HD), value.dtype)
    return pl.pallas_call(kernel, out_shape=shape, name="spread_heads")(value)


def collect_heads(value, planes):
    rows = value.shape[1]

    def kernel(in_ref, out_ref):
        for x, y, c, two in itertools.product((0, 1), repeat=4):
            start = (((x * 2 + c) * 2 + two) * 2 + y) * HD
            piece = in_ref[(x * 2 + y) * 2 + c, :, two * HD : (two + 1) * HD]
            out_ref[:, start : start + HD] = piece.astype(F32)

    shape = jax.ShapeDtypeStruct((rows, HEADS * HD), F32)
    return pl.pallas_call(kernel, out_shape=shape, name="collect_heads")(value)


def spread_units(value, planes):
    rows, count = value.shape
    hidden = count // (8 * planes)
    if hidden % HD:
        value = value.reshape(rows, 2, planes, 2, 2, hidden).transpose(2, 4, 0, 1, 3, 5)
        return value.reshape(2 * planes, rows, 4 * hidden)

    def kernel(in_ref, out_ref):
        for x, z, y, c in itertools.product((0, 1), range(planes), (0, 1), (0, 1)):
            start = (((x * planes + z) * 2 + y) * 2 + c) * hidden
            to = (x * 2 + y) * hidden
            out_ref[z * 2 + c, :, to : to + hidden] = in_ref[:, start : start + hidden]

    shape = jax.ShapeDtypeStruct((2 * planes, rows, 4 * hidden), value.dtype)
    return pl.pallas_call(kernel, out_shape=shape, name="spread_units")(value)


def collect_units(value, planes):
    _, rows, count = value.shape
    hidden = count // 4
    if hidden % HD:
        value = value.reshape(planes, 2, rows, 2, 2, hidden).transpose(2, 3, 0, 4, 1, 5)
        return value.reshape(rows, -1).astype(F32)

    def kernel(in_ref, out_ref):
        for x, z, y, c in itertools.product((0, 1), range(planes), (0, 1), (0, 1)):
            start = (((x * planes + z) * 2 + y) * 2 + c) * hidden
            at = (x * 2 + y) * hidden
            piece = in_ref[z * 2 + c, :, at : at + hidden]
            out_ref[:, start : start + hidden] = piece.astype(F32)

    shape = jax.ShapeDtypeStruct((rows, 8 * planes * hidden), F32)
    return pl.pallas_call(kernel, out_shape=shape, name="collect_units")(value)


def scatter_sum(value, axes):
    return lax.psum_scatter(value, axes, scatter_dimension=0, tiled=True)


def own_other(value, at):
    core = lax.axis_index("c")
    own = lax.dynamic_index_in_dim(value, core, at, keepdims=False)
    return own, lax.dynamic_index_in_dim(value, 1 - core, at, keepdims=False)


def in_order(own, got, at=0):
    first = lax.axis_index("c") == 0
    return jnp.stack([jnp.where(first, own, got), jnp.where(first, got, own)], axis=at)


def shift_z(value, by):
    count = lax.axis_size("z")
    return lax.ppermute(value, "z", [(i, (i + by) % count) for i in range(count)])


def line(value, pairs):
    return lax.ppermute(value, "z", pairs)


NEAR = [(0, 1), (1, 0), (2, 3), (3, 2)]
FAR = [(0, 2), (2, 0), (1, 3), (3, 1)]
MIDDLE = [(1, 2), (2, 1)]
ACROSS = [(0, 3), (3, 0), (1, 2), (2, 1)]
INWARD = [(0, 1), (3, 2)]
OUTWARD = [(1, 0), (2, 3)]


def gather_line(value):
    count = lax.axis_size("z")
    if count == 4:
        near, far = line(value, NEAR), line(value, FAR)
        middle = line(after(value, far), MIDDLE)
        pieces = [value, near, far, middle + line(far, OUTWARD)]
    else:
        pieces = [value] + [shift_z(value, step) for step in range(1, count)]
    return jnp.concatenate(pieces)


def add_cores(value):
    half = value.shape[0] // 2
    return add_low(value[:half], swap(value[half:], "c"))


def scatter_line_parts(whole):
    count = lax.axis_size("z")
    pieces = jnp.split(whole, count)
    if count == 4:
        inward = line(pieces[3], INWARD)
        middle = line(pieces[3], MIDDLE)
        outer = add_low(pieces[2], inward)

        def final():
            return [pieces[0], line(after(pieces[1], inward), NEAR), middle, line(outer, FAR)]

        return [outer, middle], final
    return [], lambda: [pieces[0]] + [shift_z(pieces[k], -k) for k in range(1, count)]


def scatter_line(value):
    count = lax.axis_size("z")
    pieces = jnp.split(value, count)
    if count == 4:
        got = [line(piece, pairs) for piece, pairs in zip(pieces[1:], (NEAR, FAR, ACROSS))]
    else:
        got = [shift_z(pieces[step], -step) for step in range(1, count)]
    total = pieces[0].astype(F32)
    for piece in got:
        total = total + piece.astype(F32)
    return total


def gather_z_direct(value):
    count = lax.axis_size("z")
    me = lax.axis_index("z")
    held = jnp.stack([value] + [shift_z(value, step) for step in range(1, count)])
    return jnp.stack(
        [lax.dynamic_index_in_dim(held, (me - a) % count, 0, keepdims=False) for a in range(count)]
    )


def gather_chips(value):
    me = lax.axis_index("x") * 2 + lax.axis_index("y")
    held = jnp.stack([value] + [hop(value, mask) for mask in (1, 2, 3)])
    return jnp.stack(
        [lax.dynamic_index_in_dim(held, me ^ a, 0, keepdims=False) for a in range(4)]
    )


def scatter_chips(value):
    pieces = jnp.split(value, 4)
    total = pieces[0].astype(F32)
    for mask in (1, 2, 3):
        total = total + hop(pieces[mask], mask).astype(F32)
    return total


def scatter_plane(value):
    return scatter_chips(add_cores(value))


def visible_keys(key_pos_ref, query_pos_ref, start_ref):
    key_pos = key_pos_ref[...]
    return (key_pos <= query_pos_ref[...]) & (key_pos >= start_ref[0])


def attention_kernel(q_ref, kv_ref, key_pos_ref, query_pos_ref, start_ref, out_ref, lse_ref):
    count = key_pos_ref.shape[0]
    queries = q_ref[...].reshape(-1, q_ref.shape[-1])
    pairs = kv_ref[...].reshape(count, 2 * HD)
    keys = pairs[:, :HD]
    values_t = pairs[:, HD:].T
    seen = visible_keys(key_pos_ref, query_pos_ref, start_ref)
    outs = []
    for head in range(queries.shape[1] // HD):
        scores = dot(keys, queries[:, head * HD : (head + 1) * HD], ((1,), (1,)))
        scores = jnp.where(seen, scores * (HD**-0.5 * LOG2E), MASKED)
        top = jnp.max(scores, axis=0, keepdims=True)
        weights = jnp.exp2(scores - top)
        total = jnp.sum(weights, axis=0, keepdims=True)
        probs = (weights * (1.0 / total)).astype(LOW)
        outs.append(dot(values_t, probs).T)
        lse_ref[0, head] = top + jnp.log2(total)
    out_ref[...] = jnp.concatenate(outs, axis=1).astype(LOW).reshape(out_ref.shape)


def attention_grad_kernel(
    q_ref, grad_ref, kv_ref, lse_ref, key_pos_ref, query_pos_ref, start_ref, dq_ref, dkv_ref
):
    count = key_pos_ref.shape[0]
    queries = q_ref[...].reshape(-1, q_ref.shape[-1])
    grads = grad_ref[...].reshape(-1, q_ref.shape[-1])
    pairs = kv_ref[...].reshape(count, 2 * HD)
    keys, values = pairs[:, :HD], pairs[:, HD:]
    keys_t = keys.T
    seen = visible_keys(key_pos_ref, query_pos_ref, start_ref)
    outs, grad_keys, grad_values = [], None, None
    for head in range(queries.shape[1] // HD):
        query = queries[:, head * HD : (head + 1) * HD]
        grad = grads[:, head * HD : (head + 1) * HD]
        scores = dot(keys, query, ((1,), (1,))) * (HD**-0.5 * LOG2E)
        probs = jnp.where(seen, jnp.exp2(scores - lse_ref[0, head]), 0.0)
        grad_probs = dot(values, grad, ((1,), (1,)))
        weighted = probs * grad_probs
        delta = jnp.sum(weighted, axis=0, keepdims=True)
        grad_scores = (weighted - probs * delta).astype(LOW)
        outs.append(dot(keys_t, grad_scores).T * HD**-0.5)
        keys_part = dot(grad_scores, query) * HD**-0.5
        values_part = dot(probs.astype(LOW), grad)
        grad_keys = keys_part if head == 0 else grad_keys + keys_part
        grad_values = values_part if head == 0 else grad_values + values_part
    dq_ref[...] = jnp.concatenate(outs, axis=1).astype(LOW).reshape(dq_ref.shape)
    dkv = jnp.concatenate([grad_keys, grad_values], axis=1)
    dkv_ref[...] = dkv.astype(LOW).reshape(dkv_ref.shape)


def normed_rows(near, far, gain, shift):
    count, width = near.shape
    block = count // 4

    def kernel(near_ref, far_ref, gain_ref, shift_ref, out_ref):
        def norm(ref):
            values = ref[...].astype(F32)
            out_ref[...] = layer_norm(values, gain_ref[...], shift_ref[...]).astype(LOW)

        first = pl.program_id(0) < 4
        pl.when(first)(lambda: norm(near_ref))
        pl.when(jnp.logical_not(first))(lambda: norm(far_ref))

    return pl.pallas_call(
        kernel,
        grid=(8,),
        in_specs=[
            pl.BlockSpec((block, width), lambda i: (jnp.minimum(i, 3), 0)),
            pl.BlockSpec((block, width), lambda i: (jnp.maximum(i - 4, 0), 0)),
            pl.BlockSpec((1, width), lambda i: (0, 0)),
            pl.BlockSpec((1, width), lambda i: (0, 0)),
        ],
        out_specs=pl.BlockSpec((block, width), lambda i: (i, 0)),
        out_shape=jax.ShapeDtypeStruct((2 * count, width), LOW),
        name="normed_rows",
    )(near, far, gain[None], shift[None])


def hidden_units(near, far, grad_near, grad_far, up_w, bias, down_w):
    count, width = near.shape
    units = up_w.shape[1]
    lanes = min(units, 256)

    def kernel(
        near_ref, far_ref, grad_near_ref, grad_far_ref, up_ref, bias_ref, down_ref,
        act_ref, pre_ref, sum_ref
    ):
        sums = jnp.zeros((1, lanes), F32)
        for side, (rows_ref, grads_ref) in enumerate(
            ((near_ref, grad_near_ref), (far_ref, grad_far_ref))
        ):
            at = slice(side * count, (side + 1) * count)
            value = dot(rows_ref[...], up_ref[...]) + bias_ref[...]
            grad = dot(grads_ref[...], down_ref[...], ((1,), (1,)))
            square = value * value
            bend = jnp.tanh(GELU_C * value * (1.0 + 0.044715 * square))
            upper = 0.5 * (1.0 + bend)
            act_ref[at, :] = (value * upper).astype(LOW)
            inner = GELU_C * (1.0 + 3 * 0.044715 * square)
            slope = upper + 0.5 * value * (1.0 - bend * bend) * inner
            low = (grad * slope).astype(LOW)
            pre_ref[at, :] = low
            sums = sums + jnp.sum(low.astype(F32), axis=0, keepdims=True)
        sum_ref[...] = sums

    once = pl.Buffered(1)
    tall = pl.BlockSpec((count, width), lambda j: (0, 0), pipeline_mode=once)
    out = pl.BlockSpec((2 * count, lanes), lambda j: (0, j))
    thin = pl.BlockSpec((1, lanes), lambda j: (0, j))
    return pl.pallas_call(
        kernel,
        grid=(units // lanes,),
        in_specs=[tall, tall, tall, tall]
        + [
            pl.BlockSpec((width, lanes), lambda j: (0, j)),
            thin,
            pl.BlockSpec((lanes, width), lambda j: (j, 0)),
        ],
        out_specs=[out, out, thin],
        out_shape=[
            jax.ShapeDtypeStruct((2 * count, units), LOW),
            jax.ShapeDtypeStruct((2 * count, units), LOW),
            jax.ShapeDtypeStruct((1, units), F32),
        ],
        compiler_params=pltpu.CompilerParams(**PARAMS),
        cost_estimate=pl.CostEstimate(
            flops=8 * count * width * units,
            bytes_accessed=8 * count * width + 4 * width * units + 8 * count * units,
            transcendentals=2 * count * units,
        ),
        name="hidden_units",
    )(near, far, grad_near, grad_far, up_w, bias[None], down_w)


def attention_specs(rows, planes, width):
    query = pl.BlockSpec((2, 1, 2, 1, rows, width), lambda i, j: (0, i, 0, j, 0, 0))
    pairs = pl.BlockSpec(
        (2, 1, 2, planes, 1, rows, 2 * HD), lambda i, j: (0, i, 0, 0, j, 0, 0)
    )
    key_pos = pl.BlockSpec((4 * planes * rows, 1), lambda i, j: (0, 0))
    query_pos = pl.BlockSpec((1, 4 * rows), lambda i, j: (0, 0))
    start = pl.BlockSpec((1, 1, 4 * rows), lambda i, j: (2 * i + j, 0, 0))
    lse = pl.BlockSpec((1, width // HD, 1, 4 * rows), lambda i, j: (2 * i + j, 0, 0, 0))
    return query, pairs, key_pos, query_pos, start, lse


PARAMS = dict(vmem_limit_bytes=60 * 2**20)


def attention(queries, pairs, key_pos, query_pos, starts):
    rows, width = queries.shape[-2:]
    planes = pairs.shape[3]
    query, pair, kpos, qpos, start, lse = attention_specs(rows, planes, width)
    area = 4 * 4 * rows * 4 * planes * rows * (width // HD)
    return pl.pallas_call(
        attention_kernel,
        grid=(2, 2),
        in_specs=[query, pair, kpos, qpos, start],
        out_specs=[query, lse],
        out_shape=[
            jax.ShapeDtypeStruct(queries.shape, LOW),
            jax.ShapeDtypeStruct((4, width // HD, 1, 4 * rows), F32),
        ],
        compiler_params=pltpu.CompilerParams(**PARAMS),
        cost_estimate=pl.CostEstimate(
            flops=4 * area * HD, bytes_accessed=pairs.size * 2 + queries.size * 4, transcendentals=area
        ),
        name="attention",
    )(queries, pairs, key_pos, query_pos, starts)


def attention_grad(queries, grads, pairs, lses, key_pos, query_pos, starts):
    rows, width = queries.shape[-2:]
    planes = pairs.shape[3]
    query, pair, kpos, qpos, start, lse = attention_specs(rows, planes, width)
    area = 4 * 4 * rows * 4 * planes * rows * (width // HD)
    return pl.pallas_call(
        attention_grad_kernel,
        grid=(2, 2),
        in_specs=[query, query, pair, lse, kpos, qpos, start],
        out_specs=[query, pair],
        out_shape=[
            jax.ShapeDtypeStruct(queries.shape, LOW),
            jax.ShapeDtypeStruct(pairs.shape, LOW),
        ],
        compiler_params=pltpu.CompilerParams(**PARAMS),
        cost_estimate=pl.CostEstimate(
            flops=area, bytes_accessed=queries.size, transcendentals=0
        ),
        name="attention_grad",
    )(queries, grads, pairs, lses, key_pos, query_pos, starts)


def local(
    tokens,
    doc_lengths,
    ln1_gain,
    ln1_shift,
    q_weight,
    q_bias,
    kv_weight,
    v_bias,
    o_weight,
    o_bias,
    ln2_gain,
    ln2_shift,
    fc_weight,
    fc_bias,
    proj_weight,
    proj_bias,
    cotangent,
):
    seqs_here, span_rows, width = tokens.shape
    row_count = seqs_here * span_rows
    planes = lax.axis_size("z")
    devices = 8 * planes
    rows = q_weight.shape[0]
    hidden = proj_weight.shape[0]
    at_x, at_z, at_y, at_c = (lax.axis_index(name) for name in ("x", "z", "y", "c"))

    small = (ln1_gain, ln1_shift, q_bias, o_bias, ln2_gain, ln2_shift, proj_bias)
    lengths = doc_lengths.reshape(-1)
    lanes = kv_weight.shape[1]
    tail = jnp.concatenate([v_bias, (lengths // 256).astype(LOW), (lengths % 256).astype(LOW)])
    lines = [jnp.pad(jnp.stack(small), ((0, 0), (0, lanes - rows)))]
    for piece in (fc_bias, tail):
        lines.append(jnp.pad(piece, (0, lanes - piece.shape[0]))[None])
    lines.append(jnp.zeros((16 - len(small) - 2, lanes), LOW))
    flat = jnp.concatenate(lines)
    packed = gather_z_direct(jnp.concatenate([kv_weight, flat]))
    packed = gather_chips(packed)
    packed = in_order(packed, swap(packed, "c"), 2)
    packed = packed.reshape(2, 2, *packed.shape[1:]).transpose(0, 2, 1, 3, 4, 5)
    pair_w = packed[..., :rows, :].reshape(width, lanes)
    flat = packed[..., rows:, :].reshape(devices, 16, lanes)
    parts = flat[:, : len(small), :rows].transpose(1, 0, 2).reshape(len(small), width).astype(F32)
    gain_one, shift_one, query_b, out_b, gain_two, shift_two, down_b = parts
    up_b = flat[:, len(small), :hidden].reshape(2, planes, 2, 2, hidden).astype(F32)
    up_b = lax.dynamic_slice(
        up_b, (0, at_z, 0, at_c, 0), (2, 1, 2, 1, hidden)
    ).reshape(-1)
    flat = flat[:, len(small) + 1]
    ends = v_bias.shape[0]
    value_b = flat[:, :ends].reshape(-1).astype(F32)
    lengths = flat[:: devices // 2, ends:].astype(jnp.int32)
    count = doc_lengths.size
    lengths = (lengths[:, :count] * 256 + lengths[:, count : 2 * count]).reshape(-1, doc_lengths.shape[1])

    up_own = exchange(spread_units(fc_weight, planes), LINE)
    own_q = after(spread_heads(q_weight, planes), up_own)
    query_w = exchange(own_q, EVERY).reshape(width, 2 * HD)
    query_b = lax.dynamic_slice(
        query_b.reshape(2, 2, 2, 2, HD), (at_x, at_c, 0, at_y, 0), (1, 1, 2, 1, HD)
    ).reshape(-1)
    whole_heads = planes == 4 and 2 * rows == HD
    if whole_heads:
        out_w = lax.all_gather(o_weight, "z", axis=0, tiled=True)
        own, other = own_other(out_w.reshape(2, 2, rows, width), 0)
        out_w = in_order(own, swap(other, "c"), 1).reshape(2 * HD, width)
    else:
        out_w = lax.all_gather(o_weight, EVERY, axis=0, tiled=True)
        out_w = lax.dynamic_slice(
            out_w.reshape(2, 2, 2, 2, HD, width),
            (at_x, at_c, 0, at_y, 0, 0),
            (1, 1, 2, 1, HD, width),
        ).reshape(2 * HD, width)

    up_w = lax.all_gather(up_own.reshape(-1, 4 * hidden), CHIPS, axis=0, tiled=True)
    down_w = lax.all_gather(proj_weight, CHIPS, axis=0, tiled=True)

    def features_out(value):
        order = [(x * planes + z) * 2 + y for x in (0, 1) for y in (0, 1) for z in range(planes)]
        return pick_blocks(value, order)

    def features_back(value):
        order = [(x * 2 + y) * planes + z for x in (0, 1) for z in range(planes) for y in (0, 1)]
        return pick_blocks(value, order)

    tokens_own = tokens.reshape(row_count, width)
    inputs_float = tokens_own.astype(F32)
    steps = jnp.arange(2, dtype=jnp.int32)
    within = jnp.arange(span_rows, dtype=jnp.int32)
    depth = (at_z - jnp.arange(planes, dtype=jnp.int32)) % planes
    core_part = (steps ^ at_c) * span_rows
    row_part = (steps ^ at_y) * (2 * span_rows)
    key_pos = (
        core_part[:, None, None, None]
        + row_part[None, :, None, None]
        + depth[None, None, :, None] * (4 * span_rows)
        + within
    ).reshape(-1, 1)
    query_pos = (
        core_part[:, None, None] + row_part[None, :, None] + at_z * (4 * span_rows) + within
    ).reshape(1, -1)
    starts = jnp.zeros((2 * seqs_here, query_pos.shape[1]), jnp.int32)
    for j in range(lengths.shape[1]):
        doc_end = jnp.sum(lengths[:, : j + 1], axis=1, keepdims=True)
        starts = jnp.where(query_pos >= doc_end, jnp.maximum(starts, doc_end), starts)
    starts = jnp.where(at_x == 0, starts, jnp.roll(starts, seqs_here, axis=0))[:, None, :]

    grad_out = cotangent.reshape(row_count, width)
    tokens_near = jnp.concatenate([tokens_own] + [hop(tokens_own, mask) for mask in (1, 2, 3)])
    normed_one_plane = normed_rows(tokens_near, swap(tokens_near, "c"), gain_one, shift_one)
    normed_one_f, norm_pull_one = jax.vjp(layer_norm, inputs_float, gain_one, shift_one)
    normed_one = normed_one_f.astype(LOW)
    pair_shift = jnp.concatenate([jnp.zeros((HD,), F32), value_b])
    pairs = (dot(normed_one, pair_w) + pair_shift).astype(LOW)
    pairs = pairs.reshape(seqs_here, span_rows, 2 * HD)
    pairs = jnp.stack([pairs] + [shift_z(pairs, step) for step in range(1, planes)])
    pairs, normed_one_plane = lax.optimization_barrier((pairs, normed_one_plane))
    pairs = jnp.stack([pairs] + [hop(pairs, mask) for mask in (1, 2, 3)])
    pairs = jnp.stack([pairs, swap(pairs, "c")])
    pairs = pairs.reshape(2, 2, 2, *pairs.shape[2:])

    plane_shape = (2, 2, 2, 2, span_rows, 2 * HD)
    queries = (dot(normed_one_plane, query_w) + query_b).astype(LOW).reshape(plane_shape)
    attn_low, lses = attention(queries, pairs, key_pos, query_pos, starts)
    attn_low = attn_low.reshape(-1, 2 * HD)
    resid = inputs_float + scatter_plane(dot(attn_low, out_w).astype(LOW)) + out_b

    grad_near = gather_line(after(grad_out, attn_low))
    grad_far = swap(grad_near, "c")
    normed_two_f, norm_pull_two = jax.vjp(layer_norm, resid, gain_two, shift_two)
    near = gather_line(features_out(normed_two_f.astype(LOW)))
    far = swap(near, "c")
    activation, grad_pre, grad_up_b = hidden_units(
        near, far, grad_near, grad_far, up_w, up_b, down_w
    )
    grad_normed_two = dot(grad_pre, up_w, ((1,), (1,))).astype(LOW)
    grad_normed_two = add_cores(grad_normed_two)
    grad_pre = after(grad_pre, grad_normed_two)
    grad_up_part = dot(jnp.concatenate([near, far]), grad_pre, ((0,), (0,))).astype(LOW)
    grad_up_w = scatter_sum(grad_up_part, CHIPS).reshape(2 * planes, rows, 4 * hidden)
    activation = after(activation, grad_up_part, grad_normed_two)
    grad_out_line = jnp.concatenate([grad_near, grad_far])
    grad_down_part = dot(activation, grad_out_line, ((0,), (0,))).astype(LOW)
    result = add_cores(dot(activation, down_w).astype(LOW))
    grad_normed_two = after(scatter_line(grad_normed_two), grad_down_part, result)
    grad_normed_two = features_back(grad_normed_two)
    grad_down_b = jnp.sum(grad_out.astype(F32), axis=0)

    grad_resid_part, grad_gain_two, grad_shift_two = norm_pull_two(grad_normed_two)
    grad_resid = grad_out.astype(F32) + grad_resid_part
    grad_proj = grad_resid.astype(LOW)

    inner, final = scatter_line_parts(after(result, grad_proj))
    grad_proj_plane = jnp.concatenate([grad_proj] + [hop(grad_proj, mask) for mask in (1, 2, 3)])
    grad_proj_plane = after(grad_proj_plane, *inner)
    grad_proj_plane = jnp.concatenate([grad_proj_plane, swap(grad_proj_plane, "c")])
    grad_down_w = scatter_sum(after(grad_down_part, grad_up_w), CHIPS).astype(F32)
    result = final()
    grad_heads = dot(grad_proj_plane, out_w, ((1,), (1,))).astype(LOW).reshape(plane_shape)
    grad_out_b = jnp.sum(grad_proj.astype(F32), axis=0)
    query_grad, grad_pairs = attention_grad(
        queries, grad_heads, pairs, lses, key_pos, query_pos, starts
    )
    query_grad = query_grad.reshape(-1, 2 * HD)
    grad_normed_one = dot(query_grad, query_w, ((1,), (1,))).astype(LOW)
    grad_pairs = add_low(grad_pairs[0], swap(grad_pairs[1], "c"))
    grad_pairs = after(grad_pairs, grad_down_w)
    grad_pairs, grad_normed_one = lax.optimization_barrier((grad_pairs, grad_normed_one))
    grad_total = grad_pairs[0, 0].astype(F32)
    for mask in (1, 2, 3):
        grad_total = grad_total + hop(grad_pairs[mask >> 1, mask & 1], mask).astype(F32)
    grad_up_w = exchange(grad_up_w, LINE)
    grad_total = after(grad_total, grad_up_w)
    output = (resid + sum(part.astype(F32) for part in result) + down_b).astype(LOW)
    grad_normed_one = add_cores(grad_normed_one)
    grad_normed_one = scatter_chips(grad_normed_one)
    grad_query_w = dot(normed_one_plane, after(query_grad, grad_total), ((0,), (0,))).astype(LOW)
    grad_query_w = lax.psum_scatter(
        grad_query_w.reshape(2, planes * 4 * rows, 2 * HD), "z", scatter_dimension=1, tiled=True
    )
    grad_pairs = after(grad_total.astype(LOW), grad_normed_one, *result)
    own_pairs = grad_pairs[0].astype(F32)
    for step in range(1, planes):
        own_pairs = own_pairs + shift_z(grad_pairs[step], -step).astype(F32)
    own_pairs = own_pairs.astype(LOW).reshape(row_count, 2 * HD)
    grad_query_b = jnp.sum(query_grad.astype(F32), axis=0)
    grad_out_w = dot(attn_low, after(grad_proj_plane, grad_normed_one), ((0,), (0,))).astype(LOW)
    if whole_heads:
        own, other = own_other(grad_out_w.reshape(2, 2, rows, width), 1)
        grad_out_w = in_order(own, swap(other, "c"), 0).reshape(planes * rows, width)
        grad_out_w = lax.psum_scatter(grad_out_w, "z", scatter_dimension=0, tiled=True).astype(F32)
    else:
        placed = lax.dynamic_update_slice(
            jnp.zeros((2, 2, 2, 2, HD, width), LOW),
            grad_out_w.reshape(1, 1, 2, 1, HD, width),
            (at_x, at_c, 0, at_y, 0, 0),
        ).reshape(width, width)
        grad_out_w = lax.psum_scatter(
            placed, EVERY, scatter_dimension=0, tiled=True
        ).astype(F32)
    grad_pair_w = dot(normed_one, own_pairs, ((0,), (0,))).astype(LOW)
    grad_value_b = jnp.sum(own_pairs[:, HD:].astype(F32), axis=0)
    grad_normed_one = grad_normed_one + dot(own_pairs, pair_w, ((1,), (1,)))
    grad_input_part, grad_gain_one, grad_shift_one = norm_pull_one(grad_normed_one)
    input_grad = grad_resid + grad_input_part

    grad_query_whole = lax.dynamic_update_slice(
        jnp.zeros((2, 2, 2, 2, HD), F32),
        grad_query_b.reshape(1, 1, 2, 1, HD),
        (at_x, at_c, 0, at_y, 0),
    ).reshape(-1)
    grad_up_whole = lax.dynamic_update_slice(
        jnp.zeros((2, planes, 2, 2, hidden), F32),
        grad_up_b.reshape(2, 1, 2, 1, hidden),
        (0, at_z, 0, at_c, 0),
    ).reshape(-1)
    vectors = (
        grad_gain_one,
        grad_shift_one,
        grad_query_whole,
        grad_out_b,
        grad_gain_two,
        grad_shift_two,
        grad_down_b,
        grad_up_whole,
        grad_value_b,
    )
    shares = [vector.reshape(devices, -1) for vector in vectors]
    lines = [jnp.pad(share, ((0, 0), (0, lanes - share.shape[1]))) for share in shares]
    flat = jnp.pad(jnp.stack(lines, axis=1), ((0, 0), (0, 16 - len(lines)), (0, 0))).astype(LOW)
    flat = jnp.concatenate([grad_pair_w.reshape(devices, rows, 2 * HD), flat], axis=1)
    flat = exchange(flat, EVERY)
    grad_query_w = exchange(after(grad_query_w.reshape(8, rows, 2 * HD), flat), PLANE)
    grad_query_w = collect_heads(grad_query_w, planes)
    flat = jnp.sum(flat.astype(F32), axis=0)
    grad_up_w = collect_units(grad_up_w, planes)
    grad_pair_w = flat[:rows]
    sums = [flat[rows + i, : share.shape[1]] for i, share in enumerate(shares)]
    return (
        output.reshape(seqs_here, span_rows, width),
        input_grad.reshape(seqs_here, span_rows, width),
        sums[0],
        sums[1],
        grad_query_w,
        sums[2],
        grad_pair_w,
        sums[8],
        grad_out_w,
        sums[3],
        sums[4],
        sums[5],
        grad_up_w,
        sums[7],
        grad_down_w,
        sums[6],
    )


def solution(mesh):
    span = mesh.shape["span"]
    fine = Mesh(mesh.devices.reshape(2, span // 4, 2, 2), ("x", "z", "y", "c"))
    every = ("x", "z", "y", "c")
    acts = P("x", ("z", "y", "c"), None)
    vector = P(every)
    matrix = P(every, None)
    return jax.shard_map(
        local,
        mesh=fine,
        in_specs=(
            acts,
            P("x", None),
            vector,
            vector,
            matrix,
            vector,
            matrix,
            vector,
            matrix,
            vector,
            vector,
            vector,
            matrix,
            vector,
            matrix,
            vector,
            acts,
        ),
        out_specs=(
            acts,
            acts,
            vector,
            vector,
            matrix,
            vector,
            matrix,
            vector,
            matrix,
            vector,
            vector,
            vector,
            matrix,
            vector,
            matrix,
            vector,
        ),
        check_vma=False,
    )
```

```python
import itertools

import jax
import jax.numpy as jnp
from jax import lax
from jax.experimental import pallas as pl
from jax.experimental.pallas import tpu as pltpu
from jax.sharding import Mesh
from jax.sharding import PartitionSpec as P

HEADS = 16
HD = 128

EPS = 1e-05
GELU_C = 0.7978845608028654
MASKED = -1e30
LOG2E = 1.4426950408889634
LOW = jnp.bfloat16
F32 = jnp.float32
SWAP = [(0, 1), (1, 0)]


def layer_norm(values, gain, shift):
    center = values - jnp.mean(values, axis=-1, keepdims=True)
    spread = jnp.mean(center * center, axis=-1, keepdims=True)
    return center * lax.rsqrt(spread + EPS) * gain + shift


def gelu_tanh(values):
    return 0.5 * values * (1.0 + jnp.tanh(GELU_C * (values + 0.044715 * values * values * values)))


def dot(left, right, dims=((1,), (0,))):
    return lax.dot_general(left, right, (dims, ((), ())), preferred_element_type=F32)


def swap(value, axis):
    return lax.ppermute(value, axis, SWAP)


def add_low(own, got):
    return (own.astype(F32) + got.astype(F32)).astype(LOW)


CHIPS = ("x", "y")
LINE = ("z", "c")
PLANE = ("x", "y", "c")
EVERY = ("x", "z", "y", "c")


def exchange(value, axes):
    return lax.all_to_all(value, axes, 0, 0, tiled=True)


def spread(value, axes):
    return exchange(jnp.broadcast_to(value, (lax.axis_size(axes), *value.shape)), axes)


def after(value, *events):
    return lax.optimization_barrier((value, *events))[0]


def hop(value, mask):
    return lax.ppermute(value, CHIPS, [(i, i ^ mask) for i in range(4)])


def pick_blocks(value, order):
    size = value.shape[1] // len(order)
    if size % HD:
        return jnp.concatenate([value[:, i * size : (i + 1) * size] for i in order], axis=1)

    def kernel(in_ref, out_ref):
        for to, i in enumerate(order):
            out_ref[:, to * size : (to + 1) * size] = in_ref[:, i * size : (i + 1) * size]

    shape = jax.ShapeDtypeStruct(value.shape, value.dtype)
    return pl.pallas_call(kernel, out_shape=shape, name="pick_blocks")(value)


def spread_heads(value, planes):
    rows = value.shape[0]

    def kernel(in_ref, out_ref):
        for x, y, c, two in itertools.product((0, 1), repeat=4):
            start = (((x * 2 + c) * 2 + two) * 2 + y) * HD
            piece = in_ref[:, start : start + HD]
            for z in range(planes):
                target = ((x * planes + z) * 2 + y) * 2 + c
                out_ref[target, :, two * HD : (two + 1) * HD] = piece

    shape = jax.ShapeDtypeStruct((8 * planes, rows, 2 * HD), value.dtype)
    return pl.pallas_call(kernel, out_shape=shape, name="spread_heads")(value)


def collect_heads(value, planes):
    rows = value.shape[1]

    def kernel(in_ref, out_ref):
        for x, y, c, two in itertools.product((0, 1), repeat=4):
            start = (((x * 2 + c) * 2 + two) * 2 + y) * HD
            piece = in_ref[(x * 2 + y) * 2 + c, :, two * HD : (two + 1) * HD]
            out_ref[:, start : start + HD] = piece.astype(F32)

    shape = jax.ShapeDtypeStruct((rows, HEADS * HD), F32)
    return pl.pallas_call(kernel, out_shape=shape, name="collect_heads")(value)


def spread_units(value, planes):
    rows, count = value.shape
    hidden = count // (8 * planes)
    if hidden % HD:
        value = value.reshape(rows, 2, planes, 2, 2, hidden).transpose(2, 4, 0, 1, 3, 5)
        return value.reshape(2 * planes, rows, 4 * hidden)

    def kernel(in_ref, out_ref):
        for x, z, y, c in itertools.product((0, 1), range(planes), (0, 1), (0, 1)):
            start = (((x * planes + z) * 2 + y) * 2 + c) * hidden
            to = (x * 2 + y) * hidden
            out_ref[z * 2 + c, :, to : to + hidden] = in_ref[:, start : start + hidden]

    shape = jax.ShapeDtypeStruct((2 * planes, rows, 4 * hidden), value.dtype)
    return pl.pallas_call(kernel, out_shape=shape, name="spread_units")(value)


def collect_units(value, planes):
    _, rows, count = value.shape
    hidden = count // 4
    if hidden % HD:
        value = value.reshape(planes, 2, rows, 2, 2, hidden).transpose(2, 3, 0, 4, 1, 5)
        return value.reshape(rows, -1).astype(F32)

    def kernel(in_ref, out_ref):
        for x, z, y, c in itertools.product((0, 1), range(planes), (0, 1), (0, 1)):
            start = (((x * planes + z) * 2 + y) * 2 + c) * hidden
            at = (x * 2 + y) * hidden
            piece = in_ref[z * 2 + c, :, at : at + hidden]
            out_ref[:, start : start + hidden] = piece.astype(F32)

    shape = jax.ShapeDtypeStruct((rows, 8 * planes * hidden), F32)
    return pl.pallas_call(kernel, out_shape=shape, name="collect_units")(value)


def scatter_sum(value, axes):
    return lax.psum_scatter(value, axes, scatter_dimension=0, tiled=True)


def own_other(value, at):
    core = lax.axis_index("c")
    own = lax.dynamic_index_in_dim(value, core, at, keepdims=False)
    return own, lax.dynamic_index_in_dim(value, 1 - core, at, keepdims=False)


def in_order(own, got, at=0):
    first = lax.axis_index("c") == 0
    return jnp.stack([jnp.where(first, own, got), jnp.where(first, got, own)], axis=at)


def shift_z(value, by):
    count = lax.axis_size("z")
    return lax.ppermute(value, "z", [(i, (i + by) % count) for i in range(count)])


def line(value, pairs):
    return lax.ppermute(value, "z", pairs)


NEAR = [(0, 1), (1, 0), (2, 3), (3, 2)]
FAR = [(0, 2), (2, 0), (1, 3), (3, 1)]
MIDDLE = [(1, 2), (2, 1)]
ACROSS = [(0, 3), (3, 0), (1, 2), (2, 1)]
INWARD = [(0, 1), (3, 2)]
OUTWARD = [(1, 0), (2, 3)]


def gather_line(value):
    count = lax.axis_size("z")
    if count == 4:
        near, far = line(value, NEAR), line(value, FAR)
        middle = line(after(value, far), MIDDLE)
        pieces = [value, near, far, middle + line(far, OUTWARD)]
    else:
        pieces = [value] + [shift_z(value, step) for step in range(1, count)]
    return jnp.concatenate(pieces)


def add_cores(value):
    half = value.shape[0] // 2
    return add_low(value[:half], swap(value[half:], "c"))


def scatter_line_parts(whole):
    count = lax.axis_size("z")
    pieces = jnp.split(whole, count)
    if count == 4:
        inward = line(pieces[3], INWARD)
        middle = line(pieces[3], MIDDLE)
        outer = add_low(pieces[2], inward)

        def final():
            return [pieces[0], line(after(pieces[1], inward), NEAR), middle, line(outer, FAR)]

        return [outer, middle], final
    return [], lambda: [pieces[0]] + [shift_z(pieces[k], -k) for k in range(1, count)]


def scatter_line(value):
    count = lax.axis_size("z")
    pieces = jnp.split(value, count)
    if count == 4:
        got = [line(piece, pairs) for piece, pairs in zip(pieces[1:], (NEAR, FAR, ACROSS))]
    else:
        got = [shift_z(pieces[step], -step) for step in range(1, count)]
    total = pieces[0].astype(F32)
    for piece in got:
        total = total + piece.astype(F32)
    return total


def gather_z_direct(value):
    count = lax.axis_size("z")
    me = lax.axis_index("z")
    held = jnp.stack([value] + [shift_z(value, step) for step in range(1, count)])
    return jnp.stack(
        [lax.dynamic_index_in_dim(held, (me - a) % count, 0, keepdims=False) for a in range(count)]
    )


def gather_chips(value):
    me = lax.axis_index("x") * 2 + lax.axis_index("y")
    held = jnp.stack([value] + [hop(value, mask) for mask in (1, 2, 3)])
    return jnp.stack(
        [lax.dynamic_index_in_dim(held, me ^ a, 0, keepdims=False) for a in range(4)]
    )


def scatter_chips(value):
    pieces = jnp.split(value, 4)
    total = pieces[0].astype(F32)
    for mask in (1, 2, 3):
        total = total + hop(pieces[mask], mask).astype(F32)
    return total


def scatter_plane(value):
    return scatter_chips(add_cores(value))


def visible_keys(key_pos_ref, query_pos_ref, start_ref):
    key_pos = key_pos_ref[...]
    return (key_pos <= query_pos_ref[...]) & (key_pos >= start_ref[0])


def attention_kernel(q_ref, kv_ref, key_pos_ref, query_pos_ref, start_ref, out_ref, lse_ref):
    count = key_pos_ref.shape[0]
    queries = q_ref[...].reshape(-1, q_ref.shape[-1])
    pairs = kv_ref[...].reshape(count, 2 * HD)
    keys = pairs[:, :HD]
    values_t = pairs[:, HD:].T
    seen = visible_keys(key_pos_ref, query_pos_ref, start_ref)
    outs = []
    for head in range(queries.shape[1] // HD):
        scores = dot(keys, queries[:, head * HD : (head + 1) * HD], ((1,), (1,)))
        scores = jnp.where(seen, scores * (HD**-0.5 * LOG2E), MASKED)
        top = jnp.max(scores, axis=0, keepdims=True)
        weights = jnp.exp2(scores - top)
        total = jnp.sum(weights, axis=0, keepdims=True)
        probs = (weights * (1.0 / total)).astype(LOW)
        outs.append(dot(values_t, probs).T)
        lse_ref[0, head] = top + jnp.log2(total)
    out_ref[...] = jnp.concatenate(outs, axis=1).astype(LOW).reshape(out_ref.shape)


def attention_grad_kernel(
    q_ref, grad_ref, kv_ref, lse_ref, key_pos_ref, query_pos_ref, start_ref, dq_ref, dkv_ref
):
    count = key_pos_ref.shape[0]
    queries = q_ref[...].reshape(-1, q_ref.shape[-1])
    grads = grad_ref[...].reshape(-1, q_ref.shape[-1])
    pairs = kv_ref[...].reshape(count, 2 * HD)
    keys, values = pairs[:, :HD], pairs[:, HD:]
    keys_t = keys.T
    seen = visible_keys(key_pos_ref, query_pos_ref, start_ref)
    outs, grad_keys, grad_values = [], None, None
    for head in range(queries.shape[1] // HD):
        query = queries[:, head * HD : (head + 1) * HD]
        grad = grads[:, head * HD : (head + 1) * HD]
        scores = dot(keys, query, ((1,), (1,))) * (HD**-0.5 * LOG2E)
        probs = jnp.where(seen, jnp.exp2(scores - lse_ref[0, head]), 0.0)
        grad_probs = dot(values, grad, ((1,), (1,)))
        weighted = probs * grad_probs
        delta = jnp.sum(weighted, axis=0, keepdims=True)
        grad_scores = (weighted - probs * delta).astype(LOW)
        outs.append(dot(keys_t, grad_scores).T * HD**-0.5)
        keys_part = dot(grad_scores, query) * HD**-0.5
        values_part = dot(probs.astype(LOW), grad)
        grad_keys = keys_part if head == 0 else grad_keys + keys_part
        grad_values = values_part if head == 0 else grad_values + values_part
    dq_ref[...] = jnp.concatenate(outs, axis=1).astype(LOW).reshape(dq_ref.shape)
    dkv = jnp.concatenate([grad_keys, grad_values], axis=1)
    dkv_ref[...] = dkv.astype(LOW).reshape(dkv_ref.shape)


def normed_rows(near, far, gain, shift):
    count, width = near.shape
    block = count // 4

    def kernel(near_ref, far_ref, gain_ref, shift_ref, out_ref):
        def norm(ref):
            values = ref[...].astype(F32)
            out_ref[...] = layer_norm(values, gain_ref[...], shift_ref[...]).astype(LOW)

        first = pl.program_id(0) < 4
        pl.when(first)(lambda: norm(near_ref))
        pl.when(jnp.logical_not(first))(lambda: norm(far_ref))

    return pl.pallas_call(
        kernel,
        grid=(8,),
        in_specs=[
            pl.BlockSpec((block, width), lambda i: (jnp.minimum(i, 3), 0)),
            pl.BlockSpec((block, width), lambda i: (jnp.maximum(i - 4, 0), 0)),
            pl.BlockSpec((1, width), lambda i: (0, 0)),
            pl.BlockSpec((1, width), lambda i: (0, 0)),
        ],
        out_specs=pl.BlockSpec((block, width), lambda i: (i, 0)),
        out_shape=jax.ShapeDtypeStruct((2 * count, width), LOW),
        name="normed_rows",
    )(near, far, gain[None], shift[None])


def hidden_units(near, far, grad_near, grad_far, up_w, bias, down_w):
    count, width = near.shape
    units = up_w.shape[1]
    lanes = min(units, 256)

    def kernel(
        near_ref, far_ref, grad_near_ref, grad_far_ref, up_ref, bias_ref, down_ref,
        act_ref, pre_ref, sum_ref
    ):
        sums = jnp.zeros((1, lanes), F32)
        for side, (rows_ref, grads_ref) in enumerate(
            ((near_ref, grad_near_ref), (far_ref, grad_far_ref))
        ):
            at = slice(side * count, (side + 1) * count)
            value = dot(rows_ref[...], up_ref[...]) + bias_ref[...]
            grad = dot(grads_ref[...], down_ref[...], ((1,), (1,)))
            square = value * value
            bend = jnp.tanh(GELU_C * value * (1.0 + 0.044715 * square))
            upper = 0.5 * (1.0 + bend)
            act_ref[at, :] = (value * upper).astype(LOW)
            inner = GELU_C * (1.0 + 3 * 0.044715 * square)
            slope = upper + 0.5 * value * (1.0 - bend * bend) * inner
            low = (grad * slope).astype(LOW)
            pre_ref[at, :] = low
            sums = sums + jnp.sum(low.astype(F32), axis=0, keepdims=True)
        sum_ref[...] = sums

    once = pl.Buffered(1)
    tall = pl.BlockSpec((count, width), lambda j: (0, 0), pipeline_mode=once)
    out = pl.BlockSpec((2 * count, lanes), lambda j: (0, j))
    thin = pl.BlockSpec((1, lanes), lambda j: (0, j))
    return pl.pallas_call(
        kernel,
        grid=(units // lanes,),
        in_specs=[tall, tall, tall, tall]
        + [
            pl.BlockSpec((width, lanes), lambda j: (0, j)),
            thin,
            pl.BlockSpec((lanes, width), lambda j: (j, 0)),
        ],
        out_specs=[out, out, thin],
        out_shape=[
            jax.ShapeDtypeStruct((2 * count, units), LOW),
            jax.ShapeDtypeStruct((2 * count, units), LOW),
            jax.ShapeDtypeStruct((1, units), F32),
        ],
        compiler_params=pltpu.CompilerParams(**PARAMS),
        cost_estimate=pl.CostEstimate(
            flops=8 * count * width * units,
            bytes_accessed=8 * count * width + 4 * width * units + 8 * count * units,
            transcendentals=2 * count * units,
        ),
        name="hidden_units",
    )(near, far, grad_near, grad_far, up_w, bias[None], down_w)


def attention_specs(rows, planes, width):
    query = pl.BlockSpec((2, 1, 2, 1, rows, width), lambda i, j: (0, i, 0, j, 0, 0))
    pairs = pl.BlockSpec(
        (2, 1, 2, planes, 1, rows, 2 * HD), lambda i, j: (0, i, 0, 0, j, 0, 0)
    )
    key_pos = pl.BlockSpec((4 * planes * rows, 1), lambda i, j: (0, 0))
    query_pos = pl.BlockSpec((1, 4 * rows), lambda i, j: (0, 0))
    start = pl.BlockSpec((1, 1, 4 * rows), lambda i, j: (2 * i + j, 0, 0))
    lse = pl.BlockSpec((1, width // HD, 1, 4 * rows), lambda i, j: (2 * i + j, 0, 0, 0))
    return query, pairs, key_pos, query_pos, start, lse


PARAMS = dict(vmem_limit_bytes=60 * 2**20)


def attention(queries, pairs, key_pos, query_pos, starts):
    rows, width = queries.shape[-2:]
    planes = pairs.shape[3]
    query, pair, kpos, qpos, start, lse = attention_specs(rows, planes, width)
    area = 4 * 4 * rows * 4 * planes * rows * (width // HD)
    return pl.pallas_call(
        attention_kernel,
        grid=(2, 2),
        in_specs=[query, pair, kpos, qpos, start],
        out_specs=[query, lse],
        out_shape=[
            jax.ShapeDtypeStruct(queries.shape, LOW),
            jax.ShapeDtypeStruct((4, width // HD, 1, 4 * rows), F32),
        ],
        compiler_params=pltpu.CompilerParams(**PARAMS),
        cost_estimate=pl.CostEstimate(
            flops=4 * area * HD, bytes_accessed=pairs.size * 2 + queries.size * 4, transcendentals=area
        ),
        name="attention",
    )(queries, pairs, key_pos, query_pos, starts)


def attention_grad(queries, grads, pairs, lses, key_pos, query_pos, starts):
    rows, width = queries.shape[-2:]
    planes = pairs.shape[3]
    query, pair, kpos, qpos, start, lse = attention_specs(rows, planes, width)
    area = 4 * 4 * rows * 4 * planes * rows * (width // HD)
    return pl.pallas_call(
        attention_grad_kernel,
        grid=(2, 2),
        in_specs=[query, query, pair, lse, kpos, qpos, start],
        out_specs=[query, pair],
        out_shape=[
            jax.ShapeDtypeStruct(queries.shape, LOW),
            jax.ShapeDtypeStruct(pairs.shape, LOW),
        ],
        compiler_params=pltpu.CompilerParams(**PARAMS),
        cost_estimate=pl.CostEstimate(
            flops=area, bytes_accessed=queries.size, transcendentals=0
        ),
        name="attention_grad",
    )(queries, grads, pairs, lses, key_pos, query_pos, starts)


def local(
    tokens,
    doc_lengths,
    ln1_gain,
    ln1_shift,
    q_weight,
    q_bias,
    kv_weight,
    v_bias,
    o_weight,
    o_bias,
    ln2_gain,
    ln2_shift,
    fc_weight,
    fc_bias,
    proj_weight,
    proj_bias,
    cotangent,
):
    seqs_here, span_rows, width = tokens.shape
    row_count = seqs_here * span_rows
    planes = lax.axis_size("z")
    devices = 8 * planes
    rows = q_weight.shape[0]
    hidden = proj_weight.shape[0]
    at_x, at_z, at_y, at_c = (lax.axis_index(name) for name in ("x", "z", "y", "c"))

    small = (ln1_gain, ln1_shift, q_bias, o_bias, ln2_gain, ln2_shift, proj_bias)
    lengths = doc_lengths.reshape(-1)
    lanes = kv_weight.shape[1]
    tail = jnp.concatenate([v_bias, (lengths // 256).astype(LOW), (lengths % 256).astype(LOW)])
    lines = [jnp.pad(jnp.stack(small), ((0, 0), (0, lanes - rows)))]
    for piece in (fc_bias, tail):
        lines.append(jnp.pad(piece, (0, lanes - piece.shape[0]))[None])
    lines.append(jnp.zeros((16 - len(small) - 2, lanes), LOW))
    flat = jnp.concatenate(lines)
    packed = gather_z_direct(jnp.concatenate([kv_weight, flat]))
    packed = gather_chips(packed)
    packed = in_order(packed, swap(packed, "c"), 2)
    packed = packed.reshape(2, 2, *packed.shape[1:]).transpose(0, 2, 1, 3, 4, 5)
    pair_w = packed[..., :rows, :].reshape(width, lanes)
    flat = packed[..., rows:, :].reshape(devices, 16, lanes)
    parts = flat[:, : len(small), :rows].transpose(1, 0, 2).reshape(len(small), width).astype(F32)
    gain_one, shift_one, query_b, out_b, gain_two, shift_two, down_b = parts
    up_b = flat[:, len(small), :hidden].reshape(2, planes, 2, 2, hidden).astype(F32)
    up_b = lax.dynamic_slice(
        up_b, (0, at_z, 0, at_c, 0), (2, 1, 2, 1, hidden)
    ).reshape(-1)
    flat = flat[:, len(small) + 1]
    ends = v_bias.shape[0]
    value_b = flat[:, :ends].reshape(-1).astype(F32)
    lengths = flat[:: devices // 2, ends:].astype(jnp.int32)
    count = doc_lengths.size
    lengths = (lengths[:, :count] * 256 + lengths[:, count : 2 * count]).reshape(-1, doc_lengths.shape[1])

    up_own = exchange(spread_units(fc_weight, planes), LINE)
    own_q = after(spread_heads(q_weight, planes), up_own)
    query_w = exchange(own_q, EVERY).reshape(width, 2 * HD)
    query_b = lax.dynamic_slice(
        query_b.reshape(2, 2, 2, 2, HD), (at_x, at_c, 0, at_y, 0), (1, 1, 2, 1, HD)
    ).reshape(-1)
    whole_heads = planes == 4 and 2 * rows == HD
    if whole_heads:
        out_w = lax.all_gather(o_weight, "z", axis=0, tiled=True)
        own, other = own_other(out_w.reshape(2, 2, rows, width), 0)
        out_w = in_order(own, swap(other, "c"), 1).reshape(2 * HD, width)
    else:
        out_w = lax.all_gather(o_weight, EVERY, axis=0, tiled=True)
        out_w = lax.dynamic_slice(
            out_w.reshape(2, 2, 2, 2, HD, width),
            (at_x, at_c, 0, at_y, 0, 0),
            (1, 1, 2, 1, HD, width),
        ).reshape(2 * HD, width)

    up_w = lax.all_gather(up_own.reshape(-1, 4 * hidden), CHIPS, axis=0, tiled=True)
    down_w = lax.all_gather(proj_weight, CHIPS, axis=0, tiled=True)

    def features_out(value):
        order = [(x * planes + z) * 2 + y for x in (0, 1) for y in (0, 1) for z in range(planes)]
        return pick_blocks(value, order)

    def features_back(value):
        order = [(x * 2 + y) * planes + z for x in (0, 1) for z in range(planes) for y in (0, 1)]
        return pick_blocks(value, order)

    tokens_own = tokens.reshape(row_count, width)
    inputs_float = tokens_own.astype(F32)
    steps = jnp.arange(2, dtype=jnp.int32)
    within = jnp.arange(span_rows, dtype=jnp.int32)
    depth = (at_z - jnp.arange(planes, dtype=jnp.int32)) % planes
    core_part = (steps ^ at_c) * span_rows
    row_part = (steps ^ at_y) * (2 * span_rows)
    key_pos = (
        core_part[:, None, None, None]
        + row_part[None, :, None, None]
        + depth[None, None, :, None] * (4 * span_rows)
        + within
    ).reshape(-1, 1)
    query_pos = (
        core_part[:, None, None] + row_part[None, :, None] + at_z * (4 * span_rows) + within
    ).reshape(1, -1)
    starts = jnp.zeros((2 * seqs_here, query_pos.shape[1]), jnp.int32)
    for j in range(lengths.shape[1]):
        doc_end = jnp.sum(lengths[:, : j + 1], axis=1, keepdims=True)
        starts = jnp.where(query_pos >= doc_end, jnp.maximum(starts, doc_end), starts)
    starts = jnp.where(at_x == 0, starts, jnp.roll(starts, seqs_here, axis=0))[:, None, :]

    grad_out = cotangent.reshape(row_count, width)
    tokens_near = jnp.concatenate([tokens_own] + [hop(tokens_own, mask) for mask in (1, 2, 3)])
    normed_one_plane = normed_rows(tokens_near, swap(tokens_near, "c"), gain_one, shift_one)
    normed_one_f, norm_pull_one = jax.vjp(layer_norm, inputs_float, gain_one, shift_one)
    normed_one = normed_one_f.astype(LOW)
    pair_shift = jnp.concatenate([jnp.zeros((HD,), F32), value_b])
    pairs = (dot(normed_one, pair_w) + pair_shift).astype(LOW)
    pairs = pairs.reshape(seqs_here, span_rows, 2 * HD)
    pairs = jnp.stack([pairs] + [shift_z(pairs, step) for step in range(1, planes)])
    pairs, normed_one_plane = lax.optimization_barrier((pairs, normed_one_plane))
    pairs = jnp.stack([pairs] + [hop(pairs, mask) for mask in (1, 2, 3)])
    pairs = jnp.stack([pairs, swap(pairs, "c")])
    pairs = pairs.reshape(2, 2, 2, *pairs.shape[2:])

    plane_shape = (2, 2, 2, 2, span_rows, 2 * HD)
    queries = (dot(normed_one_plane, query_w) + query_b).astype(LOW).reshape(plane_shape)
    attn_low, lses = attention(queries, pairs, key_pos, query_pos, starts)
    attn_low = attn_low.reshape(-1, 2 * HD)
    resid = inputs_float + scatter_plane(dot(attn_low, out_w).astype(LOW)) + out_b

    grad_near = gather_line(after(grad_out, attn_low))
    grad_far = swap(grad_near, "c")
    normed_two_f, norm_pull_two = jax.vjp(layer_norm, resid, gain_two, shift_two)
    near = gather_line(features_out(normed_two_f.astype(LOW)))
    far = swap(near, "c")
    activation, grad_pre, grad_up_b = hidden_units(
        near, far, grad_near, grad_far, up_w, up_b, down_w
    )
    grad_normed_two = dot(grad_pre, up_w, ((1,), (1,))).astype(LOW)
    grad_normed_two = add_cores(grad_normed_two)
    grad_pre = after(grad_pre, grad_normed_two)
    grad_up_part = dot(jnp.concatenate([near, far]), grad_pre, ((0,), (0,))).astype(LOW)
    grad_up_w = scatter_sum(grad_up_part, CHIPS).reshape(2 * planes, rows, 4 * hidden)
    activation = after(activation, grad_up_part, grad_normed_two)
    grad_out_line = jnp.concatenate([grad_near, grad_far])
    grad_down_part = dot(activation, grad_out_line, ((0,), (0,))).astype(LOW)
    result = add_cores(dot(activation, down_w).astype(LOW))
    grad_normed_two = after(scatter_line(grad_normed_two), grad_down_part, result)
    grad_normed_two = features_back(grad_normed_two)
    grad_down_b = jnp.sum(grad_out.astype(F32), axis=0)

    grad_resid_part, grad_gain_two, grad_shift_two = norm_pull_two(grad_normed_two)
    grad_resid = grad_out.astype(F32) + grad_resid_part
    grad_proj = grad_resid.astype(LOW)

    inner, final = scatter_line_parts(after(result, grad_proj))
    grad_proj_plane = jnp.concatenate([grad_proj] + [hop(grad_proj, mask) for mask in (1, 2, 3)])
    grad_proj_plane = after(grad_proj_plane, *inner)
    grad_proj_plane = jnp.concatenate([grad_proj_plane, swap(grad_proj_plane, "c")])
    grad_down_w = scatter_sum(after(grad_down_part, grad_up_w), CHIPS).astype(F32)
    result = final()
    grad_heads = dot(grad_proj_plane, out_w, ((1,), (1,))).astype(LOW).reshape(plane_shape)
    grad_out_b = jnp.sum(grad_proj.astype(F32), axis=0)
    query_grad, grad_pairs = attention_grad(
        queries, grad_heads, pairs, lses, key_pos, query_pos, starts
    )
    query_grad = query_grad.reshape(-1, 2 * HD)
    grad_normed_one = dot(query_grad, query_w, ((1,), (1,))).astype(LOW)
    grad_pairs = add_low(grad_pairs[0], swap(grad_pairs[1], "c"))
    grad_pairs = after(grad_pairs, grad_down_w)
    grad_pairs, grad_normed_one = lax.optimization_barrier((grad_pairs, grad_normed_one))
    grad_total = grad_pairs[0, 0].astype(F32)
    for mask in (1, 2, 3):
        grad_total = grad_total + hop(grad_pairs[mask >> 1, mask & 1], mask).astype(F32)
    grad_up_w = exchange(grad_up_w, LINE)
    grad_total = after(grad_total, grad_up_w)
    output = (resid + sum(part.astype(F32) for part in result) + down_b).astype(LOW)
    grad_normed_one = add_cores(grad_normed_one)
    grad_normed_one = scatter_chips(grad_normed_one)
    grad_query_w = dot(normed_one_plane, after(query_grad, grad_total), ((0,), (0,))).astype(LOW)
    grad_query_w = lax.psum_scatter(
        grad_query_w.reshape(2, planes * 4 * rows, 2 * HD), "z", scatter_dimension=1, tiled=True
    )
    grad_pairs = after(grad_total.astype(LOW), grad_normed_one, *result)
    own_pairs = grad_pairs[0].astype(F32)
    for step in range(1, planes):
        own_pairs = own_pairs + shift_z(grad_pairs[step], -step).astype(F32)
    own_pairs = own_pairs.astype(LOW).reshape(row_count, 2 * HD)
    grad_query_b = jnp.sum(query_grad.astype(F32), axis=0)
    grad_out_w = dot(attn_low, after(grad_proj_plane, grad_normed_one), ((0,), (0,))).astype(LOW)
    if whole_heads:
        own, other = own_other(grad_out_w.reshape(2, 2, rows, width), 1)
        grad_out_w = in_order(own, swap(other, "c"), 0).reshape(planes * rows, width)
        grad_out_w = lax.psum_scatter(grad_out_w, "z", scatter_dimension=0, tiled=True).astype(F32)
    else:
        placed = lax.dynamic_update_slice(
            jnp.zeros((2, 2, 2, 2, HD, width), LOW),
            grad_out_w.reshape(1, 1, 2, 1, HD, width),
            (at_x, at_c, 0, at_y, 0, 0),
        ).reshape(width, width)
        grad_out_w = lax.psum_scatter(
            placed, EVERY, scatter_dimension=0, tiled=True
        ).astype(F32)
    grad_pair_w = dot(normed_one, own_pairs, ((0,), (0,))).astype(LOW)
    grad_value_b = jnp.sum(own_pairs[:, HD:].astype(F32), axis=0)
    grad_normed_one = grad_normed_one + dot(own_pairs, pair_w, ((1,), (1,)))
    grad_input_part, grad_gain_one, grad_shift_one = norm_pull_one(grad_normed_one)
    input_grad = grad_resid + grad_input_part

    grad_query_whole = lax.dynamic_update_slice(
        jnp.zeros((2, 2, 2, 2, HD), F32),
        grad_query_b.reshape(1, 1, 2, 1, HD),
        (at_x, at_c, 0, at_y, 0),
    ).reshape(-1)
    grad_up_whole = lax.dynamic_update_slice(
        jnp.zeros((2, planes, 2, 2, hidden), F32),
        grad_up_b.reshape(2, 1, 2, 1, hidden),
        (0, at_z, 0, at_c, 0),
    ).reshape(-1)
    vectors = (
        grad_gain_one,
        grad_shift_one,
        grad_query_whole,
        grad_out_b,
        grad_gain_two,
        grad_shift_two,
        grad_down_b,
        grad_up_whole,
        grad_value_b,
    )
    shares = [vector.reshape(devices, -1) for vector in vectors]
    lines = [jnp.pad(share, ((0, 0), (0, lanes - share.shape[1]))) for share in shares]
    flat = jnp.pad(jnp.stack(lines, axis=1), ((0, 0), (0, 16 - len(lines)), (0, 0))).astype(LOW)
    flat = jnp.concatenate([grad_pair_w.reshape(devices, rows, 2 * HD), flat], axis=1)
    grad_up_w = collect_units(grad_up_w, planes)
    deep = flat.shape[1]
    flat = flat.reshape(2, planes, 2, 2, deep, lanes).transpose(0, 2, 3, 1, 4, 5)
    flat = flat.reshape(8, planes * deep, lanes)
    flat = jnp.concatenate([flat, grad_query_w.reshape(8, rows, 2 * HD)], axis=1)
    flat = exchange(flat, PLANE)
    grad_query_w = collect_heads(flat[:, planes * deep :], planes)
    flat = jnp.sum(flat[:, : planes * deep].astype(F32), axis=0).astype(LOW)
    flat = exchange(flat.reshape(planes, deep, lanes), "z")
    flat = jnp.sum(flat.astype(F32), axis=0)
    grad_pair_w = flat[:rows]
    sums = [flat[rows + i, : share.shape[1]] for i, share in enumerate(shares)]
    return (
        output.reshape(seqs_here, span_rows, width),
        input_grad.reshape(seqs_here, span_rows, width),
        sums[0],
        sums[1],
        grad_query_w,
        sums[2],
        grad_pair_w,
        sums[8],
        grad_out_w,
        sums[3],
        sums[4],
        sums[5],
        grad_up_w,
        sums[7],
        grad_down_w,
        sums[6],
    )


def solution(mesh):
    span = mesh.shape["span"]
    fine = Mesh(mesh.devices.reshape(2, span // 4, 2, 2), ("x", "z", "y", "c"))
    every = ("x", "z", "y", "c")
    acts = P("x", ("z", "y", "c"), None)
    vector = P(every)
    matrix = P(every, None)
    return jax.shard_map(
        local,
        mesh=fine,
        in_specs=(
            acts,
            P("x", None),
            vector,
            vector,
            matrix,
            vector,
            matrix,
            vector,
            matrix,
            vector,
            vector,
            vector,
            matrix,
            vector,
            matrix,
            vector,
            acts,
        ),
        out_specs=(
            acts,
            acts,
            vector,
            vector,
            matrix,
            vector,
            matrix,
            vector,
            matrix,
            vector,
            vector,
            vector,
            matrix,
            vector,
            matrix,
            vector,
        ),
        check_vma=False,
    )
```
